256 devices in a mesh: node: 32 (over z, x), rep: 8 (over y, core).
Axes of the slice: x: 4, y: 4, z: 8, core: 2. Of those that a mesh axis runs over, the one named last changes fastest.
Arguments:
- table: bfloat16 [49152, 768], P('node'), may hold values from -6 to 6
- near_owner: int32 [2048, 26, 1], P(('node', 'rep')), may hold values from 0 to 31; in each aligned block of 208 rows (0 to 207, 208 to 415, ..., all dimensions but the last counted through in order) at most 13 rows name the same one
- near_row: int32 [2048, 26], P(('node', 'rep')), may hold values from 0 to 1535
- far_owner: int32 [2048, 375, 1], P(('node', 'rep')), may hold values from 0 to 31; in each aligned block of 3000 rows (0 to 2999, 3000 to 5999, ..., all dimensions but the last counted through in order) at most 187 rows name the same one
- far_row: int32 [2048, 375], P(('node', 'rep')), may hold values from 0 to 1535
- w_self1: bfloat16 [768, 1024], replicated, may hold values from -0.21875 to 0.21875
- w_neigh1: bfloat16 [768, 1024], replicated, may hold values from -0.875 to 0.875
- w_self2: bfloat16 [1024, 153], replicated, may hold values from -0.1875 to 0.1875
- w_neigh2: bfloat16 [1024, 153], replicated, may hold values from -1 to 1
- out_grad: bfloat16 [2048, 153], P(('node', 'rep')), may hold values from -0.29882812 to 0.29882812
Outputs:
- grad_self1: bfloat16 [768, 1024], replicated
- grad_neigh1: bfloat16 [768, 1024], replicated
- grad_self2: bfloat16 [1024, 153], replicated
- grad_neigh2: bfloat16 [1024, 153], replicated
The draws below stay inside these ranges and needn't reach their ends.
Inputs may be any that keep to these rules, and one draw needn't show every extreme that they name: `near_owner`: among the rows of one device no owner is named more than 13 times, a bound that some block reaches. `far_owner`: among the rows of one device no owner is named more than 187 times, a bound that some block reaches.
All inputs are finite; a program needn't handle non-finite values.
Results may differ from the reference program's by a relative error of at most 0.013.
Values may be sent and summed in bfloat16 or wider, within the bound.
A program may use at most 128 MiB of HBM per device.

```python
import math
import jax
import jax.numpy as jnp
import numpy as np
from jax import lax

D = 768
H = 1024
C = 153
F1 = 25
F2 = 15
SEEDS_DEV = 8
ROWS_DEV = 1536
SEEDS = 2048
NODES = 49152
CAP1 = 13
CAP2 = 187
N_NODE = 32


def place_ends(result, rng, low, high):
    longest = result.shape.index(max(result.shape))
    spots = []
    for shift in (0, 1):
        where = [jax.random.randint(jax.random.fold_in(rng, axis), (), 0, length) for axis, length in enumerate(result.shape)]
        where[longest] = (where[longest] + shift) % result.shape[longest]
        spots.append(tuple(where))
    return result.at[spots[0]].set(low).at[spots[1]].set(high)


def steps_of(stream_key, shape, shards, least, high):
    factor_of, own = 1.0, jax.random.fold_in(stream_key, 6)
    for position, blocks in shards:
        steps = jnp.exp(jax.random.uniform(jax.random.fold_in(own, position), (blocks,), jnp.float32, least / len(shards), high / len(shards)))
        factor_of = factor_of * jnp.repeat(steps, shape[position] // blocks).reshape([-1 if axis == position else 1 for axis in range(len(shape))])
    return factor_of


def deal_out(own_key, own, number, rows, count, top, most, skew):
    order = jax.random.permutation(own_key, count)
    heavy_load, ordinary = shares(count, rows * top, most, skew, True), shares(count, rows * top, most, skew, False)
    places = jnp.arange(count)

    def named(lengths, rotation):
        used = int((lengths > 0).sum())
        fixed = max(1, used // 4)
        passed = fixed + (places - fixed + rotation * (used - fixed)) % max(1, count - fixed)
        return jnp.zeros((count,), jnp.int32).at[order[jnp.where(places < fixed, places, passed)]].set(jnp.asarray(lengths, jnp.int32))

    lengths = jnp.where(number % 4 == 0, named(heavy_load, number // 4), named(ordinary, number - number // 4 - 1))
    mixed = jax.random.permutation(jax.random.fold_in(own, 3), count)
    giver, taker = mixed[0:count // 2 * 2:2], mixed[1:count // 2 * 2:2]
    margin = jnp.minimum(lengths[giver] - 1, most - lengths[taker]) // 2
    margin = jnp.where((giver == order[0]) | (taker == order[0]) | (lengths[taker] == 0), 0, jnp.maximum(margin, 0))
    passed = jax.random.randint(jax.random.fold_in(own, 4), (count // 2,), 0, 1 << 20) % (margin + 1)
    lengths = lengths.at[giver].add(-passed).at[taker].add(passed)
    members = jnp.searchsorted(jnp.cumsum(lengths), jnp.arange(rows * top), side="right").astype(jnp.int32)
    table = members.reshape(top, rows).T
    table = table[jax.random.permutation(jax.random.fold_in(own, 1), rows)]
    rotation = jax.random.randint(jax.random.fold_in(own, 2), (rows, 1), 0, top)
    return jnp.take_along_axis(table, (jnp.arange(top)[None, :] + rotation) % top, axis=1)


def shares(count, total, bound, lean, full):
    loads = [(1 << 20) // math.isqrt(standing ** lean) + 1 for standing in range(1, count + 1)]
    largest = bound if full else min(bound, max(-(-total // count), total * loads[0] // sum(loads)))
    least = 1 if total - largest >= count - 1 else 0
    counts, surplus = [largest] + [least] * (count - 1), total - largest - least * (count - 1)
    while surplus > 0:
        candidates = [i for i in range(1, count) if counts[i] < largest] or [i for i in range(1, count) if counts[i] < bound]
        mass, remaining = sum([loads[i] for i in candidates]), surplus
        for i in candidates:
            extra = min(bound - counts[i], max(1, remaining * loads[i] // mass), surplus)
            counts[i] = counts[i] + extra
            surplus = surplus - extra
    return np.array(counts)


def gaussian(stream_key, extent, width, limit, split=(), kind=jnp.bfloat16):
    entries = jax.random.normal(stream_key, extent, jnp.float32) * width
    if len(split) > 0:
        entries = steps_of(stream_key, extent, split, -0.22, 0.18) * entries
    return jnp.clip(entries, min=-limit, max=limit).astype(kind)


def setup_inputs(seed: int = 0) -> dict:
    key_of = jax.random.split(jax.random.key(seed), 11)
    table = gaussian(key_of[0], (NODES, D), 1.0, 6.0, ((0, 32),))
    near_owner_keys = jax.random.split(jax.random.fold_in(key_of[1], 1), SEEDS * (1 + F1) // (SEEDS_DEV * (1 + F1)))
    near_owner_turns = jax.random.permutation(jax.random.fold_in(key_of[1], 3), SEEDS * (1 + F1) // (SEEDS_DEV * (1 + F1)))
    near_owner = jax.vmap(lambda own, number: deal_out(jax.random.fold_in(key_of[1], 2), own, number, SEEDS_DEV * (1 + F1), N_NODE, 1, CAP1, 2))(near_owner_keys, near_owner_turns).reshape((SEEDS, 1 + F1, 1))
    near_row = place_ends(jax.random.randint(key_of[2], (SEEDS, 1 + F1), 0, ROWS_DEV), jax.random.fold_in(key_of[2], 1), 0, ROWS_DEV - 1).astype(jnp.int32)
    far_owner_keys = jax.random.split(jax.random.fold_in(key_of[3], 1), SEEDS * (F1 * F2) // (SEEDS_DEV * F1 * F2))
    far_owner_turns = jax.random.permutation(jax.random.fold_in(key_of[3], 3), SEEDS * (F1 * F2) // (SEEDS_DEV * F1 * F2))
    far_owner = jax.vmap(lambda own, number: deal_out(jax.random.fold_in(key_of[3], 2), own, number, SEEDS_DEV * F1 * F2, N_NODE, 1, CAP2, 2))(far_owner_keys, far_owner_turns).reshape((SEEDS, F1 * F2, 1))
    far_row = place_ends(jax.random.randint(key_of[4], (SEEDS, F1 * F2), 0, ROWS_DEV), jax.random.fold_in(key_of[4], 1), 0, ROWS_DEV - 1).astype(jnp.int32)
    w_self1 = gaussian(key_of[5], (D, H), D ** -0.5, 0.21875)
    w_neigh1 = gaussian(key_of[6], (D, H), (D // F2) ** -0.5, 0.875)
    w_self2 = gaussian(key_of[7], (H, C), H ** -0.5, 0.1875)
    w_neigh2 = gaussian(key_of[8], (H, C), (H // F1) ** -0.5, 1.0)
    out_grad = gaussian(key_of[9], (SEEDS, C), 0.05, 0.29882812, ((0, 256),))
    return dict(table=table, near_owner=near_owner, near_row=near_row, far_owner=far_owner, far_row=far_row, w_self1=w_self1, w_neigh1=w_neigh1, w_self2=w_self2, w_neigh2=w_neigh2, out_grad=out_grad)


def silu_slope(value):
    sigma = 1.0 / (1.0 + jnp.exp(-value))
    return sigma * (1.0 + value * (1.0 - sigma))


def far_block(table, owners, rows):
    ids = owners * ROWS_DEV + rows
    feats = table[ids].astype(jnp.float32).reshape(SEEDS_DEV, F1, F2, D)
    grouped = owners.reshape(SEEDS_DEV, F1, F2)
    same = grouped[..., :, None] == grouped[..., None, :]
    lower = jnp.arange(F2, dtype=jnp.int32)[None, :] < jnp.arange(F2, dtype=jnp.int32)[:, None]
    first = jnp.logical_not(jnp.any(same & lower, axis=-1)).astype(jnp.float32)
    part = jnp.einsum("stkl,stld->stkd", same.astype(jnp.float32), feats).astype(jnp.bfloat16)
    return jnp.einsum("stk,stkd->std", first, part.astype(jnp.float32))


def reference(table, near_owner, near_row, far_owner, far_row, w_self1, w_neigh1, w_self2, w_neigh2, out_grad):
    near_ids = near_owner[..., 0] * ROWS_DEV + near_row
    x_near = table[near_ids]
    x_seed = x_near[:, 0]
    x_one = x_near[:, 1:]
    mean_one = (jnp.sum(x_one.astype(jnp.float32), axis=1) / F1).astype(jnp.bfloat16)
    blocks = SEEDS // SEEDS_DEV
    owners = far_owner[..., 0].reshape(blocks, SEEDS_DEV, F1 * F2)
    rows = far_row.reshape(blocks, SEEDS_DEV, F1 * F2)
    summed = lax.map(lambda pair: far_block(table, pair[0], pair[1]), (owners, rows))
    mean_two = (summed.reshape(SEEDS * F1, D) / F2).astype(jnp.bfloat16)
    flat_one = x_one.reshape(SEEDS * F1, D)
    pre_seed = jnp.dot(x_seed, w_self1, preferred_element_type=jnp.float32) + jnp.dot(mean_one, w_neigh1, preferred_element_type=jnp.float32)
    pre_one = jnp.dot(flat_one, w_self1, preferred_element_type=jnp.float32) + jnp.dot(mean_two, w_neigh1, preferred_element_type=jnp.float32)
    h_seed = jax.nn.silu(pre_seed).astype(jnp.bfloat16)
    h_one = jax.nn.silu(pre_one).astype(jnp.bfloat16)
    mean_h = (jnp.sum(h_one.astype(jnp.float32).reshape(SEEDS, F1, H), axis=1) / F1).astype(jnp.bfloat16)
    grad_self2 = jnp.dot(h_seed.T, out_grad, preferred_element_type=jnp.float32)
    grad_neigh2 = jnp.dot(mean_h.T, out_grad, preferred_element_type=jnp.float32)
    d_seed = jnp.dot(out_grad, w_self2.T, preferred_element_type=jnp.float32)
    d_mean = jnp.dot(out_grad, w_neigh2.T, preferred_element_type=jnp.float32)
    g_seed = (d_seed * silu_slope(pre_seed)).astype(jnp.bfloat16)
    spread = jnp.repeat(d_mean / F1, F1, axis=0)
    g_one = (spread * silu_slope(pre_one)).astype(jnp.bfloat16)
    grad_self1 = jnp.dot(x_seed.T, g_seed, preferred_element_type=jnp.float32) + jnp.dot(flat_one.T, g_one, preferred_element_type=jnp.float32)
    grad_neigh1 = jnp.dot(mean_one.T, g_seed, preferred_element_type=jnp.float32) + jnp.dot(mean_two.T, g_one, preferred_element_type=jnp.float32)
    return (grad_self1.astype(jnp.bfloat16), grad_neigh1.astype(jnp.bfloat16), grad_self2.astype(jnp.bfloat16), grad_neigh2.astype(jnp.bfloat16))
```

```python
import jax, jax.numpy as jnp
from jax import lax
from jax.sharding import PartitionSpec as P
from jax.experimental import pallas as pl
from jax.experimental.pallas import tpu as pltpu
MESH = pl.DeviceIdType.MESH
NZ, NX, REP = 8, 4, 8
ROWS, W = 1536, 96
F1, F2 = 25, 15
G4 = ROWS // 4
UNITS = ((0, 80), (80, 80), (160, 112), (272, 112))


def plan():
    msgs = []
    def hops(size, half):
        out = []
        for h in range(1, size // 2 + 1):
            for d in (1, -1):
                if 2 * h == size and (d == 1) != (half == 0):
                    continue
                out.append((h, d))
        return out
    for u in range(4):
        half = u % 2
        first, second = ("x", "z") if u < 2 else ("z", "x")
        size = {"x": NX, "z": NZ}
        reach = [(0, 0)]
        for h, d in hops(size[first], half):
            off = {first: -h * d, second: 0}
            msgs.append((h, u, off["x"], off["z"], first, d))
            reach.append((-h * d, h))
        for o, base in reach:
            for h, d in hops(size[second], half):
                off = {first: o, second: -h * d}
                msgs.append((base + h, u, off["x"], off["z"], second, d))
    msgs.sort(key=lambda m: m[0])
    return msgs


PLAN = plan()


def fetch_kernel(idx_ref, table_ref, out_ref, land, t32, sums, ones, stage, idx_land, idx_smem,
                 send_sem, recv_sem, isend, irecv, osend, orecv, lsem):
    node, rep = lax.axis_index("node"), lax.axis_index("rep")
    z, x = node // NX, node % NX

    def at(dx, dz):
        return ((z + dz + 2 * NZ) % NZ) * NX + (x + dx + 2 * NX) % NX

    barrier = pltpu.get_barrier_semaphore()
    for n in (at(1, 0), at(-1, 0), at(0, 1), at(0, -1)):
        pl.semaphore_signal(barrier, inc=1, device_id=(n, rep), device_id_type=MESH)
    for k in range(1, REP):
        pl.semaphore_signal(barrier, inc=1, device_id=(node, (rep + k) % REP), device_id_type=MESH)

    c = lax.broadcasted_iota(jnp.int32, (768, 384), 0)
    d = lax.broadcasted_iota(jnp.int32, (768, 384), 1)
    j = d // 128
    hit = c == rep * W + j * 32 + d % 32
    group = jnp.where(hit, ((d // 32) % 4 - j + 4) % 4, -1)
    acc = jnp.zeros((G4, 384), jnp.float32)
    for g in range(4):
        perm = jnp.where(group == g, 1.0, 0.0).astype(jnp.bfloat16)
        acc = acc + jnp.dot(table_ref[g * G4:(g + 1) * G4, :], perm, preferred_element_type=jnp.float32)
    land[node] = acc.astype(jnp.bfloat16)
    pl.semaphore_wait(barrier, 4 + REP - 1)

    def icopy(k):
        return pltpu.make_async_remote_copy(src_ref=idx_ref, dst_ref=idx_land.at[rep], send_sem=isend.at[k], recv_sem=irecv.at[k],
                                            device_id=(node, (rep + k) % REP), device_id_type=MESH)
    for k in range(1, REP):
        icopy(k).start()
    idx_land[rep] = idx_ref[...]

    def slot(u, n):
        return land.at[n, pl.ds(UNITS[u][0], UNITS[u][1])]

    def send(m, i):
        _, u, ox, oz, axis, dr = m
        sx, sz = (ox + dr, oz) if axis == "x" else (ox, oz + dr)
        to = at(dr, 0) if axis == "x" else at(0, dr)
        s = slot(u, at(sx, sz))
        return pltpu.make_async_remote_copy(src_ref=s, dst_ref=s, send_sem=send_sem.at[i], recv_sem=recv_sem.at[i],
                                            device_id=(to, rep), device_id_type=MESH)

    def arrival(m, i):
        _, u, ox, oz, axis, dr = m
        s = slot(u, at(ox, oz))
        return pltpu.make_async_remote_copy(src_ref=s, dst_ref=s, send_sem=send_sem.at[i], recv_sem=recv_sem.at[i],
                                            device_id=(node, (rep + 1) % REP), device_id_type=MESH)

    lane = lax.broadcasted_iota(jnp.int32, (16, 128), 1) // 32

    def unpack(n):
        def body(i, _):
            r0 = pl.multiple_of(i * 16, 16)
            p = land[n, pl.ds(r0, 16), :].astype(jnp.float32)
            ps = [p[:, 128 * q:128 * q + 128] for q in range(3)]
            for g in range(4):
                s = jnp.where(lane == g, ps[0], jnp.where(lane == (g + 1) % 4, ps[1], jnp.where(lane == (g + 2) % 4, ps[2], 0.0)))
                if g:
                    s = pltpu.roll(s, 128 - 32 * g, 1)
                t32[pl.ds(pl.multiple_of(n * ROWS + g * G4 + r0, 16), 16), :] = s
            return 0
        lax.fori_loop(0, G4 // 16, body, 0)

    def start_children(u, ox, oz, started):
        for i, m in enumerate(PLAN):
            if m[1] != u or i in started:
                continue
            sx, sz = (m[2] + m[5], m[3]) if m[4] == "x" else (m[2], m[3] + m[5])
            if (sx % NX, sz % NZ) == (ox % NX, oz % NZ):
                started.add(i)
                send(m, i).start()

    started = set()
    for u in range(4):
        start_children(u, 0, 0, started)
    last = max(m[0] for m in PLAN)
    unpack(node)
    for k in range(1, REP):
        icopy(k).wait_recv()
    cp = pltpu.make_async_copy(idx_land, idx_smem, lsem)
    cp.start()
    for t in range(1, last + 1):
        seen = []
        for i, m in enumerate(PLAN):
            if m[0] != t:
                continue
            arrival(m, i).wait_recv()
            start_children(m[1], m[2], m[3], started)
            if (m[2] % NX, m[3] % NZ) not in seen:
                seen.append((m[2] % NX, m[3] % NZ))
        for ox, oz in seen:
            unpack(at(ox, oz))
    assert len(started) == len(PLAN)
    cp.wait()

    def ocopy(k):
        return pltpu.make_async_remote_copy(src_ref=stage.at[k], dst_ref=out_ref.at[rep], send_sem=osend.at[k], recv_sem=orecv.at[k],
                                            device_id=(node, (rep + k) % REP), device_id_type=MESH)

    for k in list(range(1, REP)) + [0]:
        p = (rep + k) % REP

        def body(i, _):
            for u in range(8):
                def row(q):
                    return t32[pl.ds(idx_smem[p, i, 16 * u + q], 1), :]
                rows = [row(q) for q in range(15)]
                while len(rows) > 1:
                    rows = [rows[a] + rows[a + 1] if a + 1 < len(rows) else rows[a] for a in range(0, len(rows), 2)]
                sums[pl.ds(i * 8 + u, 1), :] = rows[0]
                ones[pl.ds(i * 8 + u, 1), :] = row(15)
            return 0
        lax.fori_loop(0, 25, body, 0)
        for u in range(8):
            ones[pl.ds(200 + u, 1), :] = t32[pl.ds(idx_smem[p, 25, u], 1), :]
        sums[200:208, :] = jnp.zeros((8, 128), jnp.float32)
        for h, part in ((0, (sums[...] / 15.0)), (1, ones[...])):
            if k:
                stage[k, 208 * h:208 * h + 208, :] = part.astype(jnp.bfloat16)
            else:
                out_ref[rep, 208 * h:208 * h + 208, :] = part.astype(jnp.bfloat16)
        if k:
            ocopy(k).start()
    for k in range(1, REP):
        ocopy(k).wait()
        icopy(k).wait_send()
    for i, m in enumerate(PLAN):
        send(m, i).wait_send()


def fetch(idx, table):
    n = len(PLAN)
    return pl.pallas_call(
        fetch_kernel,
        out_shape=jax.ShapeDtypeStruct((REP, 416, 128), jnp.bfloat16),
        in_specs=[pl.BlockSpec(memory_space=pltpu.VMEM)] * 2,
        out_specs=pl.BlockSpec(memory_space=pltpu.VMEM),
        scratch_shapes=[
            pltpu.VMEM((NZ * NX, G4, 384), jnp.bfloat16),
            pltpu.VMEM((NZ * NX * ROWS, 128), jnp.float32),
            pltpu.VMEM((208, 128), jnp.float32),
            pltpu.VMEM((208, 128), jnp.float32),
            pltpu.VMEM((REP, 416, 128), jnp.bfloat16),
            pltpu.VMEM((REP, 32, 128), jnp.int32),
            pltpu.SMEM((REP, 32, 128), jnp.int32),
            pltpu.SemaphoreType.DMA((n,)),
            pltpu.SemaphoreType.DMA((n,)),
            pltpu.SemaphoreType.DMA((REP,)),
            pltpu.SemaphoreType.DMA((REP,)),
            pltpu.SemaphoreType.DMA((REP,)),
            pltpu.SemaphoreType.DMA((REP,)),
            pltpu.SemaphoreType.DMA,
        ],
        compiler_params=pltpu.CompilerParams(collective_id=0, has_side_effects=True, vmem_limit_bytes=56 * 2**20),
        cost_estimate=pl.CostEstimate(flops=10**9, bytes_accessed=10**7, transcendentals=0),
        name="fetch",
    )(idx, table)


def build_idx(near_owner, near_row, far_owner, far_row):
    near = near_owner[..., 0] * ROWS + near_row
    far = far_owner[..., 0] * ROWS + far_row
    pairs = jnp.concatenate([far.reshape(200, 15), near[:, 1:].reshape(200, 1)], axis=1).reshape(25, 128)
    seed = jnp.pad(near[:, :1].reshape(1, 8), ((0, 0), (0, 120)))
    return jnp.concatenate([pairs, seed, jnp.zeros((6, 128), jnp.int32)], axis=0)


def silu_slope(value):
    sigma = 1.0 / (1.0 + jnp.exp(-value))
    return sigma * (1.0 + value * (1.0 - sigma))


def per_device(
    table, near_owner, near_row, far_owner, far_row, w_self1, w_neigh1, w_self2, w_neigh2, out_grad
):
    seeds, hidden = 8, w_self1.shape[1]
    got = fetch(build_idx(near_owner, near_row, far_owner, far_row), table)
    got = got[:, :, :W].transpose(1, 0, 2).reshape(416, REP * W)
    mean_two, x_one, x_seed = got[:200], got[208:408], got[408:]
    mean_one = (jnp.sum(x_one.reshape(seeds, F1, -1), axis=1, dtype=jnp.float32) / F1).astype(jnp.bfloat16)
    x_all = got[208:]
    m_all = jnp.concatenate([mean_two, mean_one], axis=0)
    pre = jnp.dot(x_all, w_self1, preferred_element_type=jnp.float32) + jnp.dot(
        m_all, w_neigh1, preferred_element_type=jnp.float32
    )
    h = jax.nn.silu(pre).astype(jnp.bfloat16)
    h_seed = h[200:]
    mean_h = (jnp.sum(h[:200].reshape(seeds, F1, hidden), axis=1, dtype=jnp.float32) / F1).astype(jnp.bfloat16)
    grad_self2 = jnp.dot(h_seed.T, out_grad, preferred_element_type=jnp.float32)
    grad_neigh2 = jnp.dot(mean_h.T, out_grad, preferred_element_type=jnp.float32)
    d_seed = jnp.dot(out_grad, w_self2.T, preferred_element_type=jnp.float32)
    d_mean = jnp.dot(out_grad, w_neigh2.T, preferred_element_type=jnp.float32)
    d_all = jnp.concatenate([jnp.repeat(d_mean / F1, F1, axis=0), d_seed], axis=0)
    g = (d_all * silu_slope(pre)).astype(jnp.bfloat16)
    grad_self1 = jnp.dot(x_all.T, g, preferred_element_type=jnp.float32)
    grad_neigh1 = jnp.dot(m_all.T, g, preferred_element_type=jnp.float32)
    grads = lax.psum((grad_self1, grad_neigh1, grad_self2, grad_neigh2), ("node", "rep"))
    return tuple(v.astype(jnp.bfloat16) for v in grads)


def solution(mesh):
    rows = P(("node", "rep"))
    return jax.shard_map(
        per_device,
        mesh=mesh,
        in_specs=(P("node"), rows, rows, rows, rows, P(), P(), P(), P(), rows),
        out_specs=(P(), P(), P(), P()),
        check_vma=False,
    )
```

```python
import jax, jax.numpy as jnp
from jax import lax
from jax.sharding import PartitionSpec as P
from jax.experimental import pallas as pl
from jax.experimental.pallas import tpu as pltpu
MESH = pl.DeviceIdType.MESH
NZ, NX, REP = 8, 4, 8
ROWS, W = 1536, 96
G4 = ROWS // 4
UNITS = ((0, 80), (80, 80), (160, 112), (272, 112))


def plan():
    msgs = []
    def hops(size, half):
        out = []
        for h in range(1, size // 2 + 1):
            for d in (1, -1):
                if 2 * h == size and (d == 1) != (half == 0):
                    continue
                out.append((h, d))
        return out
    for u in range(4):
        half = u % 2
        first, second = ("x", "z") if u < 2 else ("z", "x")
        size = {"x": NX, "z": NZ}
        reach = [(0, 0)]
        for h, d in hops(size[first], half):
            off = {first: -h * d, second: 0}
            msgs.append((h, u, off["x"], off["z"], first, d))
            reach.append((-h * d, h))
        for o, base in reach:
            for h, d in hops(size[second], half):
                off = {first: o, second: -h * d}
                msgs.append((base + h, u, off["x"], off["z"], second, d))
    msgs.sort(key=lambda m: m[0])
    return msgs


PLAN = plan()


def fetch_kernel(idx_ref, table_ref, out_ref, land, t32, sums, ones, stage, idx_land, idx_smem,
                 send_sem, recv_sem, isend, irecv, osend, orecv, lsem):
    node, rep = lax.axis_index("node"), lax.axis_index("rep")
    z, x = node // NX, node % NX

    def at(dx, dz):
        return ((z + dz + 2 * NZ) % NZ) * NX + (x + dx + 2 * NX) % NX

    barrier = pltpu.get_barrier_semaphore()
    for n in (at(1, 0), at(-1, 0), at(0, 1), at(0, -1)):
        pl.semaphore_signal(barrier, inc=1, device_id=(n, rep), device_id_type=MESH)
    for k in range(1, REP):
        pl.semaphore_signal(barrier, inc=1, device_id=(node, (rep + k) % REP), device_id_type=MESH)

    c = lax.broadcasted_iota(jnp.int32, (768, 384), 0)
    d = lax.broadcasted_iota(jnp.int32, (768, 384), 1)
    j = d // 128
    hit = c == rep * W + j * 32 + d % 32
    group = jnp.where(hit, ((d // 32) % 4 - j + 4) % 4, -1)
    acc = jnp.zeros((G4, 384), jnp.float32)
    for g in range(4):
        perm = jnp.where(group == g, 1.0, 0.0).astype(jnp.bfloat16)
        acc = acc + jnp.dot(table_ref[g * G4:(g + 1) * G4, :], perm, preferred_element_type=jnp.float32)
    land[node] = acc.astype(jnp.bfloat16)
    pl.semaphore_wait(barrier, 4 + REP - 1)

    def icopy(k):
        return pltpu.make_async_remote_copy(src_ref=idx_ref, dst_ref=idx_land.at[rep], send_sem=isend.at[k], recv_sem=irecv.at[k],
                                            device_id=(node, (rep + k) % REP), device_id_type=MESH)
    for k in range(1, REP):
        icopy(k).start()
    idx_land[rep] = idx_ref[...]

    def slot(u, n):
        return land.at[n, pl.ds(UNITS[u][0], UNITS[u][1])]

    def send(m, i):
        _, u, ox, oz, axis, dr = m
        sx, sz = (ox + dr, oz) if axis == "x" else (ox, oz + dr)
        to = at(dr, 0) if axis == "x" else at(0, dr)
        s = slot(u, at(sx, sz))
        return pltpu.make_async_remote_copy(src_ref=s, dst_ref=s, send_sem=send_sem.at[i], recv_sem=recv_sem.at[i],
                                            device_id=(to, rep), device_id_type=MESH)

    def arrival(m, i):
        _, u, ox, oz, axis, dr = m
        s = slot(u, at(ox, oz))
        return pltpu.make_async_remote_copy(src_ref=s, dst_ref=s, send_sem=send_sem.at[i], recv_sem=recv_sem.at[i],
                                            device_id=(node, (rep + 1) % REP), device_id_type=MESH)

    lane = lax.broadcasted_iota(jnp.int32, (16, 128), 1) // 32

    def unpack(n):
        def body(i, _):
            r0 = pl.multiple_of(i * 16, 16)
            p = land[n, pl.ds(r0, 16), :].astype(jnp.float32)
            ps = [p[:, 128 * q:128 * q + 128] for q in range(3)]
            for g in range(4):
                s = jnp.where(lane == g, ps[0], jnp.where(lane == (g + 1) % 4, ps[1], jnp.where(lane == (g + 2) % 4, ps[2], 0.0)))
                if g:
                    s = pltpu.roll(s, 128 - 32 * g, 1)
                t32[pl.ds(pl.multiple_of(n * ROWS + g * G4 + r0, 16), 16), :] = s
            return 0
        lax.fori_loop(0, G4 // 16, body, 0)

    def start_children(u, ox, oz, started):
        for i, m in enumerate(PLAN):
            if m[1] != u or i in started:
                continue
            sx, sz = (m[2] + m[5], m[3]) if m[4] == "x" else (m[2], m[3] + m[5])
            if (sx % NX, sz % NZ) == (ox % NX, oz % NZ):
                started.add(i)
                send(m, i).start()

    started = set()
    for u in range(4):
        start_children(u, 0, 0, started)
    last = max(m[0] for m in PLAN)
    unpack(node)
    for k in range(1, REP):
        icopy(k).wait_recv()
    cp = pltpu.make_async_copy(idx_land, idx_smem, lsem)
    cp.start()
    for t in range(1, last + 1):
        seen = []
        for i, m in enumerate(PLAN):
            if m[0] != t:
                continue
            arrival(m, i).wait_recv()
            start_children(m[1], m[2], m[3], started)
            if (m[2] % NX, m[3] % NZ) not in seen:
                seen.append((m[2] % NX, m[3] % NZ))
        for ox, oz in seen:
            unpack(at(ox, oz))
    assert len(started) == len(PLAN)
    cp.wait()

    def ocopy(k):
        return pltpu.make_async_remote_copy(src_ref=stage.at[k], dst_ref=out_ref.at[rep], send_sem=osend.at[k], recv_sem=orecv.at[k],
                                            device_id=(node, (rep + k) % REP), device_id_type=MESH)

    for k in list(range(1, REP)) + [0]:
        p = (rep + k) % REP

        def body(i, _):
            for u in range(8):
                def row(q):
                    return t32[pl.ds(idx_smem[p, i, 16 * u + q], 1), :]
                rows = [row(q) for q in range(15)]
                while len(rows) > 1:
                    rows = [rows[a] + rows[a + 1] if a + 1 < len(rows) else rows[a] for a in range(0, len(rows), 2)]
                sums[pl.ds(i * 8 + u, 1), :] = rows[0]
                ones[pl.ds(i * 8 + u, 1), :] = row(15)
            return 0
        lax.fori_loop(0, 25, body, 0)
        for u in range(8):
            ones[pl.ds(200 + u, 1), :] = t32[pl.ds(idx_smem[p, 25, u], 1), :]
        sums[200:208, :] = jnp.zeros((8, 128), jnp.float32)
        for h, part in ((0, (sums[...] / 15.0)), (1, ones[...])):
            if k:
                stage[k, 208 * h:208 * h + 208, :] = part.astype(jnp.bfloat16)
            else:
                out_ref[rep, 208 * h:208 * h + 208, :] = part.astype(jnp.bfloat16)
        if k:
            ocopy(k).start()
    for k in range(1, REP):
        ocopy(k).wait()
        icopy(k).wait_send()
    for i, m in enumerate(PLAN):
        send(m, i).wait_send()


def fetch(idx, table):
    n = len(PLAN)
    return pl.pallas_call(
        fetch_kernel,
        out_shape=jax.ShapeDtypeStruct((REP, 416, 128), jnp.bfloat16),
        in_specs=[pl.BlockSpec(memory_space=pltpu.VMEM)] * 2,
        out_specs=pl.BlockSpec(memory_space=pltpu.VMEM),
        scratch_shapes=[
            pltpu.VMEM((NZ * NX, G4, 384), jnp.bfloat16),
            pltpu.VMEM((NZ * NX * ROWS, 128), jnp.float32),
            pltpu.VMEM((208, 128), jnp.float32),
            pltpu.VMEM((208, 128), jnp.float32),
            pltpu.VMEM((REP, 416, 128), jnp.bfloat16),
            pltpu.VMEM((REP, 32, 128), jnp.int32),
            pltpu.SMEM((REP, 32, 128), jnp.int32),
            pltpu.SemaphoreType.DMA((n,)),
            pltpu.SemaphoreType.DMA((n,)),
            pltpu.SemaphoreType.DMA((REP,)),
            pltpu.SemaphoreType.DMA((REP,)),
            pltpu.SemaphoreType.DMA((REP,)),
            pltpu.SemaphoreType.DMA((REP,)),
            pltpu.SemaphoreType.DMA,
        ],
        compiler_params=pltpu.CompilerParams(collective_id=0, has_side_effects=True, vmem_limit_bytes=56 * 2**20),
        cost_estimate=pl.CostEstimate(flops=10**9, bytes_accessed=10**7, transcendentals=0),
        name="fetch",
    )(idx, table)


def build_idx(near_owner, near_row, far_owner, far_row):
    near = near_owner[..., 0] * ROWS + near_row
    far = far_owner[..., 0] * ROWS + far_row
    pairs = jnp.concatenate([far.reshape(200, 15), near[:, 1:].reshape(200, 1)], axis=1).reshape(25, 128)
    seed = jnp.pad(near[:, :1].reshape(1, 8), ((0, 0), (0, 120)))
    return jnp.concatenate([pairs, seed, jnp.zeros((6, 128), jnp.int32)], axis=0)


F1 = 25
WIDE = 256
ROWS_G = 2048
CP = 160
N_SEM = 2 + 2 * (6 + 6 + 7 + 7 + 4 + 4 + 4)


def step_kernel(got_ref, ws1, wn1, ws2, wn2, og_ref, fin, xs, ms, acc, sb, sib, crecv, big, small, tiny, send_sem, recv_sem):
    node, rep = lax.axis_index("node"), lax.axis_index("rep")
    z, x = node // NX, node % NX
    y, core = rep // 2, rep % 2

    def dev(axis, d):
        if axis == "x":
            return (z * NX + (x + d + NX) % NX, rep)
        if axis == "y":
            return (node, ((y + d + 4) % 4) * 2 + core)
        if axis == "z":
            return (((z + d + NZ) % NZ) * NX + x, rep)
        return (node, y * 2 + 1 - core)

    barrier = pltpu.get_barrier_semaphore()
    peers = [("x", 1), ("x", -1), ("y", 1), ("y", -1), ("c", 1)] + [("z", k) for k in range(1, NZ)]
    for a, d in peers:
        pl.semaphore_signal(barrier, inc=1, device_id=dev(a, d), device_id_type=MESH)

    counter = [0]

    def new():
        counter[0] += 1
        return counter[0] - 1

    def copy(i, src, dst, axis, d):
        return pltpu.make_async_remote_copy(src_ref=src, dst_ref=dst, send_sem=send_sem.at[i], recv_sem=recv_sem.at[i],
                                            device_id=dev(axis, d), device_id_type=MESH)
    sent = []

    def send(i, src, dst, axis, d):
        c = copy(i, src, dst, axis, d)
        c.start()
        sent.append(c)

    def arrive(i, dst):
        copy(i, dst, dst, "c", 1).wait_recv()

    for ref, lo in ((ms, 0), (xs, 208)):
        lane = lax.broadcasted_iota(jnp.int32, (208, 128), 1)
        chunks = [None] * 6
        for r in range(REP):
            q, o = 96 * r // 128, 96 * r % 128
            v = got_ref[r, lo:lo + 208, :].astype(jnp.float32)
            if o:
                v = pltpu.roll(v, o, 1)
            here = jnp.where(lane >= o, v, 0.0) if o > 32 else v
            chunks[q] = here if chunks[q] is None else chunks[q] + here
            if o > 32:
                chunks[q + 1] = jnp.where(lane < o, v, 0.0)
        for q in range(6):
            ref[:, 128 * q:128 * q + 128] = chunks[q].astype(jnp.bfloat16)
    r8 = lax.broadcasted_iota(jnp.int32, (8, 208), 0)
    c8 = lax.broadcasted_iota(jnp.int32, (8, 208), 1)
    pick = jnp.where((c8 < 200) & (c8 // F1 == r8), 1.0, 0.0).astype(jnp.bfloat16)
    mean_one = jnp.dot(pick, xs[...], preferred_element_type=jnp.float32) / F1
    ms[192:208, :] = jnp.concatenate([ms[192:208, :].astype(jnp.float32)[:8], mean_one], axis=0).astype(jnp.bfloat16)
    rr = lax.broadcasted_iota(jnp.int32, (208, 8), 0)
    cc = lax.broadcasted_iota(jnp.int32, (208, 8), 1)
    spread = jnp.where(jnp.where(rr < 200, rr // F1, rr - 200) == cc, 1.0, 0.0)
    ogs = jnp.dot(spread, og_ref[...].astype(jnp.float32), preferred_element_type=jnp.float32)
    row = lax.broadcasted_iota(jnp.int32, (208, CP), 0)
    og_one = jnp.where(row < 200, ogs, 0.0).astype(jnp.bfloat16)
    og_seed = jnp.where(row < 200, 0.0, ogs).astype(jnp.bfloat16)
    TN = (((0,), (0,)), ((), ()))
    NT = (((1,), (1,)), ((), ()))

    def grads(pair, put):
        cols = pl.ds(pl.multiple_of(pair * WIDE, WIDE), WIDE)
        pre = jnp.dot(xs[...], ws1[:, cols], preferred_element_type=jnp.float32) + jnp.dot(
            ms[...], wn1[:, cols], preferred_element_type=jnp.float32)
        s = 1.0 / (1.0 + jnp.exp(-pre))
        h = (pre * s).astype(jnp.bfloat16)
        d = lax.dot_general(og_one, wn2[cols, :], NT, preferred_element_type=jnp.float32) / F1 + lax.dot_general(
            og_seed, ws2[cols, :], NT, preferred_element_type=jnp.float32)
        g = (d * (s * (1.0 + pre * (1.0 - s)))).astype(jnp.bfloat16)
        put(0, 768, lax.dot_general(xs[...], g, TN, preferred_element_type=jnp.float32))
        put(768, 768, lax.dot_general(ms[...], g, TN, preferred_element_type=jnp.float32))
        put(1536, CP, lax.dot_general(og_seed, h, TN, preferred_element_type=jnp.float32))
        put(1536 + CP, CP, lax.dot_general(og_one, h, TN, preferred_element_type=jnp.float32) / F1)

    waited = False
    core_sem = [new(), new()]
    for part in range(2):
        def put(lo, n, v):
            for c in range(2):
                sib[part, c, lo:lo + n, :] = v[:, 128 * c:128 * c + 128].astype(jnp.bfloat16)
        grads((1 - core) * 2 + part, put)
        for c in range(2):
            sib[part, c, 1536 + 2 * CP:, :] = jnp.zeros((ROWS_G - 1536 - 2 * CP, 128), jnp.bfloat16)
        if not waited:
            pl.semaphore_wait(barrier, len(peers))
            waited = True
        send(core_sem[part], sib.at[part], crecv.at[part], "c", 1)

    def fold(part, row0, n, srcs):
        step = min(n, 64)

        def body(k, _):
            o = pl.multiple_of(k * step, 16)
            for c in range(2):
                where = pl.ds(pl.multiple_of(row0 + o, 16), step)
                v = acc[part, c, where, :]
                for ref in srcs:
                    v = v + ref[c, pl.ds(o, step), :].astype(jnp.float32)
                acc[part, c, where, :] = v
                sb[part, c, where, :] = v.astype(jnp.bfloat16)
            return 0
        lax.fori_loop(0, n // step, body, 0)

    def rows(ref, part, row0, n):
        return ref.at[part, :, pl.ds(pl.multiple_of(row0, 16), n)]

    class Ring:
        def __init__(self, part, axis, base, n, buf):
            self.part, self.axis, self.base, self.n, self.buf = part, axis, base, n, buf
            self.i = {"x": x, "y": y}[axis]
            self.sem = [new() for _ in range(6)]

        def q(self, k):
            return self.base + self.n * ((self.i + k) % 4)

        def go(self, m, row0, d):
            send(self.sem[m], rows(sb, self.part, row0, self.n // 2), self.buf.at[self.part, m], self.axis, d)

        def first(self):
            h = self.n // 2
            self.go(0, self.q(2), 1)
            self.go(2, self.q(2) + h, -1)
            self.go(1, self.q(1) + h, 1)
            self.go(3, self.q(3), -1)

        def second(self):
            h = self.n // 2
            for m, row0, d in ((0, self.q(1), 1), (2, self.q(3) + h, -1)):
                arrive(self.sem[m], self.buf.at[self.part, m])
                fold(self.part, row0, h, [self.buf.at[self.part, m]])
                self.go(4 + m // 2, row0, d)

        def last(self):
            h = self.n // 2
            for m in (3, 4, 1, 5):
                arrive(self.sem[m], self.buf.at[self.part, m])
            fold(self.part, self.q(0), h, [self.buf.at[self.part, 3], self.buf.at[self.part, 4]])
            fold(self.part, self.q(0) + h, h, [self.buf.at[self.part, 1], self.buf.at[self.part, 5]])

    axes = (("x", "y"), ("y", "x"))
    rings1 = []
    for part in range(2):
        def put(lo, n, v):
            for c in range(2):
                acc[part, c, lo:lo + n, :] = v[:, 128 * c:128 * c + 128]
        grads(core * 2 + part, put)
        for c in range(2):
            acc[part, c, 1536 + 2 * CP:, :] = jnp.zeros((ROWS_G - 1536 - 2 * CP, 128), jnp.float32)
        arrive(core_sem[part], crecv.at[part])
        fold(part, 0, ROWS_G, [crecv.at[part]])
        ring = Ring(part, axes[part][0], 0, 512, big)
        ring.first()
        rings1.append(ring)
    for ring in rings1:
        ring.second()
    rings2 = []
    for ring in rings1:
        ring.last()
        nxt = Ring(ring.part, axes[ring.part][1], ring.q(0), 128, small)
        nxt.first()
        rings2.append(nxt)
    for ring in rings2:
        ring.second()
    zsem = [[new() for _ in range(NZ - 1)] for _ in range(2)]
    for ring in rings2:
        ring.last()
        for k in range(1, NZ):
            send(zsem[ring.part][k - 1], rows(sb, ring.part, ring.q(0) + 16 * ((z + k) % NZ), 16), tiny.at[ring.part, k - 1], "z", k)

    def final(part, row0, n):
        return fin.at[pl.ds(4 * core + 2 * part, 2), pl.ds(pl.multiple_of(row0, 16), n)]

    fsem = [[new() for _ in range(NZ - 1)] for _ in range(2)]
    for ring in rings2:
        p = ring.part
        for k in range(1, NZ):
            arrive(zsem[p][k - 1], tiny.at[p, k - 1])
        r0 = pl.multiple_of(ring.q(0) + 16 * z, 16)
        for c in range(2):
            v = acc[p, c, pl.ds(r0, 16), :]
            for k in range(NZ - 1):
                v = v + tiny[p, k, c].astype(jnp.float32)
            fin[4 * core + 2 * p + c, pl.ds(r0, 16), :] = v.astype(jnp.bfloat16)
        for k in range(1, NZ):
            here = final(p, r0, 16)
            send(fsem[p][k - 1], here, here, "z", k)

    def spread_first(part, axis, base, n, i, sem):
        here = final(part, base + n * i, n)
        send(sem[0], here, here, axis, 1)
        send(sem[1], here, here, axis, -1)

    def spread_second(part, axis, base, n, i, sem):
        h = n // 2
        a = base + n * ((i + 3) % 4)
        arrive(sem[0], final(part, a, n))
        here = final(part, a, h)
        send(sem[2], here, here, axis, 1)
        b = base + n * ((i + 1) % 4)
        arrive(sem[1], final(part, b, n))
        here = final(part, b + h, h)
        send(sem[3], here, here, axis, -1)
        return a, b

    def spread_last(part, axis, base, n, i, sem):
        o = base + n * ((i + 2) % 4)
        arrive(sem[2], final(part, o, n // 2))
        arrive(sem[3], final(part, o + n // 2, n // 2))
        return o

    sems = [[new() for _ in range(4)] for _ in range(2)]
    for ring in rings2:
        for k in range(1, NZ):
            arrive(fsem[ring.part][k - 1], final(ring.part, ring.q(0) + 16 * ((z - k + NZ) % NZ), 16))
        spread_first(ring.part, ring.axis, ring.base, 128, ring.i, sems[ring.part])
    for ring in rings2:
        spread_second(ring.part, ring.axis, ring.base, 128, ring.i, sems[ring.part])
    sems1 = [[new() for _ in range(4)] for _ in range(2)]
    csem = [[new() for _ in range(4)] for _ in range(2)]

    def across(part, k, row0):
        here = final(part, row0, 512)
        send(csem[part][k], here, here, "c", 1)

    for ring in rings2:
        p = ring.part
        spread_last(p, ring.axis, ring.base, 128, ring.i, sems[p])
        spread_first(p, axes[p][0], 0, 512, rings1[p].i, sems1[p])
        across(p, 0, rings1[p].q(0))
    for ring in rings1:
        p = ring.part
        a, b = spread_second(p, ring.axis, 0, 512, ring.i, sems1[p])
        across(p, 1, a)
        across(p, 2, b)
    for ring in rings1:
        p = ring.part
        across(p, 3, spread_last(p, ring.axis, 0, 512, ring.i, sems1[p]))
    for ring in rings1:
        p = ring.part
        for k, off in enumerate((0, 3, 1, 2)):
            here = fin.at[pl.ds(4 * (1 - core) + 2 * p, 2), pl.ds(pl.multiple_of(ring.q(off), 16), 512)]
            arrive(csem[p][k], here)
    for c in sent:
        c.wait_send()
    assert counter[0] == N_SEM, counter[0]


def step(got, ws1, wn1, ws2, wn2, og):
    bf, f32 = jnp.bfloat16, jnp.float32
    return pl.pallas_call(
        step_kernel,
        out_shape=jax.ShapeDtypeStruct((8, ROWS_G, 128), bf),
        in_specs=[pl.BlockSpec(memory_space=pltpu.VMEM)] * 6,
        out_specs=pl.BlockSpec(memory_space=pltpu.VMEM),
        scratch_shapes=[
            pltpu.VMEM((208, 768), bf), pltpu.VMEM((208, 768), bf),
            pltpu.VMEM((2, 2, ROWS_G, 128), f32), pltpu.VMEM((2, 2, ROWS_G, 128), bf),
            pltpu.VMEM((2, 2, ROWS_G, 128), bf), pltpu.VMEM((2, 2, ROWS_G, 128), bf),
            pltpu.VMEM((2, 6, 2, 256, 128), bf), pltpu.VMEM((2, 6, 2, 64, 128), bf), pltpu.VMEM((2, 7, 2, 16, 128), bf),
            pltpu.SemaphoreType.DMA((N_SEM,)), pltpu.SemaphoreType.DMA((N_SEM,)),
        ],
        compiler_params=pltpu.CompilerParams(collective_id=1, has_side_effects=True, vmem_limit_bytes=56 * 2**20),
        cost_estimate=pl.CostEstimate(flops=3 * 10**9, bytes_accessed=2 * 10**7, transcendentals=0),
        name="step",
    )(got, ws1, wn1, ws2, wn2, og)


def finish(fin):
    def tall(lo):
        return fin[:, lo:lo + 768, :].transpose(1, 0, 2).reshape(768, 1024)

    def wide(lo):
        return fin[:, lo:lo + 153, :].transpose(0, 2, 1).reshape(1024, 153)
    return tall(0), tall(768), wide(1536), wide(1536 + CP)


def update(got, ws1, wn1, ws2, wn2, og):
    pad = lambda a: jnp.pad(a, ((0, 0), (0, CP - a.shape[1])))
    return finish(step(got, ws1, wn1, pad(ws2), pad(wn2), pad(og)))


def per_device(
    table, near_owner, near_row, far_owner, far_row, w_self1, w_neigh1, w_self2, w_neigh2, out_grad
):
    got = fetch(build_idx(near_owner, near_row, far_owner, far_row), table)
    return update(got, w_self1, w_neigh1, w_self2, w_neigh2, out_grad)


def solution(mesh):
    rows = P(("node", "rep"))
    return jax.shard_map(
        per_device,
        mesh=mesh,
        in_specs=(P("node"), rows, rows, rows, rows, P(), P(), P(), P(), rows),
        out_specs=(P(), P(), P(), P()),
        check_vma=False,
    )
```

```python
import jax
import jax.numpy as jnp
from jax import lax
from jax.experimental import pallas as pl
from jax.experimental.pallas import tpu as pltpu
from jax.sharding import PartitionSpec as P

MESH = pl.DeviceIdType.MESH
NZ, NX, REP = 8, 4, 8
ROWS, W = 1536, 96
F1, F2 = 25, 15
G4 = ROWS // 4
UNITS = ((0, 80), (80, 80), (160, 112), (272, 112))
WIDE = 256
ROWS_G = 2048
C = 153
GS2, GN2 = 1536, 1696
N_SEM = 2 + 2 * (6 + 6 + 7 + 7 + 4 + 4 + 4)
GROUPS = 5


def plan():
    msgs = []
    def hops(size, half):
        out = []
        for h in range(1, size // 2 + 1):
            for d in (1, -1):
                if 2 * h == size and (d == 1) != (half == 0):
                    continue
                out.append((h, d))
        return out
    for u in range(4):
        half = u % 2
        first, second = ("x", "z") if u < 2 else ("z", "x")
        size = {"x": NX, "z": NZ}
        reach = [(0, 0)]
        for h, d in hops(size[first], half):
            off = {first: -h * d, second: 0}
            msgs.append((h, u, off["x"], off["z"], first, d))
            reach.append((-h * d, h))
        for o, base in reach:
            for h, d in hops(size[second], half):
                off = {first: o, second: -h * d}
                msgs.append((base + h, u, off["x"], off["z"], second, d))
    msgs.sort(key=lambda m: m[0])
    return msgs


PLAN = plan()


def kernel(no_ref, nr_ref, fo_ref, fr_ref, table, ws1_h, wn1_h, ws2, wn2, og_ref, gs1, gn1, gs2, gn2,
           tw, land, t32, sums, ones, stage, got, idx_own, idx_land, idx_smem, ws1, wn1,
           xs, ms, sb, sib, crecv, big, small, tiny, fin,
           ag_send, ag_recv, isend, irecv, osend, orecv, send_sem, recv_sem, lsem):
    node, rep = lax.axis_index("node"), lax.axis_index("rep")
    z, x = node // NX, node % NX
    y, core = rep // 2, rep % 2
    window = pl.multiple_of(128 * jnp.minimum(3 * rep // 4, 4), 128)
    get_table = pltpu.make_async_copy(table.at[:, pl.ds(window, 256)], tw, lsem.at[0])
    get_table.start()
    get_ws1 = pltpu.make_async_copy(ws1_h, ws1, lsem.at[1])
    get_wn1 = pltpu.make_async_copy(wn1_h, wn1, lsem.at[2])
    get_ws1.start()
    get_wn1.start()

    def at(dx, dz):
        return ((z + dz + 2 * NZ) % NZ) * NX + (x + dx + 2 * NX) % NX

    def dev(axis, d):
        if axis == "x":
            return (at(d, 0), rep)
        if axis == "y":
            return (node, ((y + d + 4) % 4) * 2 + core)
        if axis == "z":
            return (at(0, d), rep)
        if axis == "rep":
            return (node, (rep + d) % REP)
        return (node, y * 2 + 1 - core)

    barrier = pltpu.get_barrier_semaphore()
    peers = [("x", 1), ("x", -1)] + [("z", k) for k in range(1, NZ)] + [("rep", k) for k in range(1, REP)]
    for axis, d in peers:
        pl.semaphore_signal(barrier, inc=1, device_id=dev(axis, d), device_id_type=MESH)

    far = fo_ref[...] * ROWS + fr_ref[...]
    near = no_ref[...] * ROWS + nr_ref[...]
    idx_own[...] = jnp.zeros_like(idx_own)
    for t in range(GROUPS):
        idx_own[t, :, 0:75] = far[:, 75 * t:75 * t + 75]
        idx_own[t, :, 75:80] = near[:, 1 + 5 * t:6 + 5 * t]
        idx_own[t, :, 80:81] = near[:, 0:1]

    c = lax.broadcasted_iota(jnp.int32, (256, 384), 0)
    d = lax.broadcasted_iota(jnp.int32, (256, 384), 1)
    j = d // 128
    hit = c == rep * W - window + j * 32 + d % 32
    group = jnp.where(hit, ((d // 32) % 4 - j + 4) % 4, -1)
    perms = [jnp.where(group == g, 1.0, 0.0).astype(jnp.bfloat16) for g in range(4)]
    get_table.wait()

    def pack(lo, n):
        acc = jnp.zeros((n, 384), jnp.float32)
        for g in range(4):
            acc = acc + jnp.dot(tw[g * G4 + lo:g * G4 + lo + n, :], perms[g], preferred_element_type=jnp.float32)
        land[node, lo:lo + n, :] = acc.astype(jnp.bfloat16)

    def slot(u, n):
        return land.at[n, pl.ds(UNITS[u][0], UNITS[u][1])]

    def ag_copy(m, i):
        _, u, ox, oz, axis, dr = m
        s = slot(u, at(ox + dr, oz) if axis == "x" else at(ox, oz + dr))
        return pltpu.make_async_remote_copy(src_ref=s, dst_ref=s, send_sem=ag_send.at[i], recv_sem=ag_recv.at[i],
                                            device_id=dev(axis, dr), device_id_type=MESH)

    def ag_arrival(m, i):
        s = slot(m[1], at(m[2], m[3]))
        return pltpu.make_async_remote_copy(src_ref=s, dst_ref=s, send_sem=ag_send.at[i], recv_sem=ag_recv.at[i],
                                            device_id=dev("rep", 1), device_id_type=MESH)

    lane = lax.broadcasted_iota(jnp.int32, (96, 128), 1) // 32

    def unpack(n, half):
        def body(i, _):
            r0 = pl.multiple_of(i * 96, 16)
            p = land[n, pl.ds(r0, 96), :].astype(jnp.float32)
            ps = [p[:, 128 * q:128 * q + 128] for q in range(3)]
            for g in range(4):
                s = jnp.where(lane == g, ps[0], jnp.where(lane == (g + 1) % 4, ps[1], jnp.where(lane == (g + 2) % 4, ps[2], 0.0)))
                if g:
                    s = pltpu.roll(s, 128 - 32 * g, 1)
                t32[pl.ds(pl.multiple_of(n * ROWS + g * G4 + r0, 16), 96), :] = s
            return 0
        lax.fori_loop(2 * half, 2 * half + 2, body, 0)

    started = set()

    def start_children(u, ox, oz):
        for i, m in enumerate(PLAN):
            if m[1] != u or i in started:
                continue
            sx, sz = (m[2] + m[5], m[3]) if m[4] == "x" else (m[2], m[3] + m[5])
            if (sx % NX, sz % NZ) == (ox % NX, oz % NZ):
                started.add(i)
                ag_copy(m, i).start()

    pack(0, 160)
    pl.semaphore_wait(barrier, len(peers))
    for u in (0, 1):
        start_children(u, 0, 0)
    pack(160, 224)
    for u in (2, 3):
        start_children(u, 0, 0)

    def icopy(k):
        return pltpu.make_async_remote_copy(src_ref=idx_own, dst_ref=idx_land.at[rep], send_sem=isend.at[k], recv_sem=irecv.at[k],
                                            device_id=dev("rep", k), device_id_type=MESH)
    for k in range(1, REP):
        icopy(k).start()
    idx_land[rep] = idx_own[...]
    work = [(0, 0, 0), (0, 0, 1)]
    for t in range(1, PLAN[-1][0] + 1):
        seen = []
        for i, m in enumerate(PLAN):
            if m[0] != t:
                continue
            ag_arrival(m, i).wait_recv()
            start_children(m[1], m[2], m[3])
            if (m[2] % NX, m[3] % NZ) not in seen:
                seen.append((m[2] % NX, m[3] % NZ))
            if work:
                ox, oz, half = work.pop(0)
                unpack(at(ox, oz), half)
        work += [(ox, oz, half) for ox, oz in seen for half in range(2)]
        if t == 2:
            for k in range(1, REP):
                icopy(k).wait_recv()
            to_smem = pltpu.make_async_copy(idx_land, idx_smem, lsem.at[3])
            to_smem.start()
    for ox, oz, half in work:
        unpack(at(ox, oz), half)
    to_smem.wait()

    def ocopy(k):
        return pltpu.make_async_remote_copy(src_ref=stage.at[k], dst_ref=got.at[rep], send_sem=osend.at[k], recv_sem=orecv.at[k],
                                            device_id=dev("rep", k), device_id_type=MESH)

    def arrived_slice(k):
        there = got.at[(rep - k + REP) % REP]
        return pltpu.make_async_remote_copy(src_ref=there, dst_ref=there, send_sem=osend.at[k], recv_sem=orecv.at[k],
                                            device_id=dev("rep", k), device_id_type=MESH)

    sums[200:208, :] = jnp.zeros((8, 128), jnp.float32)
    for k in list(range(1, REP)) + [0]:
        p = (rep + k) % REP

        def body(i, _):
            t = i // 4
            for half in range(2):
                b = i % 4 * 2 + half

                def row(q):
                    return t32[pl.ds(idx_smem[p, t, b, q], 1), :]
                for u in range(5):
                    rows = [row(u * F2 + q) for q in range(F2)]
                    while len(rows) > 1:
                        rows = [rows[a] + rows[a + 1] if a + 1 < len(rows) else rows[a] for a in range(0, len(rows), 2)]
                    sums[pl.ds(b * F1 + t * 5 + u, 1), :] = rows[0]
                    ones[pl.ds(b * F1 + t * 5 + u, 1), :] = row(75 + u)
            return 0
        lax.fori_loop(0, 4 * GROUPS, body, 0)
        for b in range(8):
            ones[pl.ds(200 + b, 1), :] = t32[pl.ds(idx_smem[p, 0, b, 80], 1), :]
        for h, part in ((0, sums[...] / F2), (1, ones[...])):
            if k:
                stage[k, 208 * h:208 * h + 208, :] = part.astype(jnp.bfloat16)
            else:
                got[rep, 208 * h:208 * h + 208, :] = part.astype(jnp.bfloat16)
        if k:
            ocopy(k).start()
    get_ws1.wait()
    get_wn1.wait()
    for k in range(1, REP):
        arrived_slice(k).wait_recv()
    counter = [0]

    def acc_row(part, c, row):
        return (2 * part + c) * ROWS_G + row

    def new():
        counter[0] += 1
        return counter[0] - 1

    def copy(i, src, dst, axis, d):
        return pltpu.make_async_remote_copy(src_ref=src, dst_ref=dst, send_sem=send_sem.at[i], recv_sem=recv_sem.at[i],
                                            device_id=dev(axis, d), device_id_type=MESH)
    sent = []

    def send(i, src, dst, axis, d):
        c = copy(i, src, dst, axis, d)
        c.start()
        sent.append(c)

    def arrive(i, dst):
        copy(i, dst, dst, "c", 1).wait_recv()

    for ref, lo in ((ms, 0), (xs, 208)):
        lane = lax.broadcasted_iota(jnp.int32, (208, 128), 1)
        chunks = [None] * 6
        for r in range(REP):
            q, o = 96 * r // 128, 96 * r % 128
            v = got[r, lo:lo + 208, :].astype(jnp.float32)
            if o:
                v = pltpu.roll(v, o, 1)
            here = jnp.where(lane >= o, v, 0.0) if o > 32 else v
            chunks[q] = here if chunks[q] is None else chunks[q] + here
            if o > 32:
                chunks[q + 1] = jnp.where(lane < o, v, 0.0)
        for q in range(6):
            ref[:, 128 * q:128 * q + 128] = chunks[q].astype(jnp.bfloat16)
    r8 = lax.broadcasted_iota(jnp.int32, (8, 208), 0)
    c8 = lax.broadcasted_iota(jnp.int32, (8, 208), 1)
    pick = jnp.where((c8 < 200) & (c8 // F1 == r8), 1.0, 0.0).astype(jnp.bfloat16)
    mean_one = jnp.dot(pick, xs[...], preferred_element_type=jnp.float32) / F1
    ms[192:208, :] = jnp.concatenate([ms[192:208, :].astype(jnp.float32)[:8], mean_one], axis=0).astype(jnp.bfloat16)
    rr = lax.broadcasted_iota(jnp.int32, (208, 8), 0)
    cc = lax.broadcasted_iota(jnp.int32, (208, 8), 1)
    spread = jnp.where(jnp.where(rr < 200, rr // F1, rr - 200) == cc, 1.0, 0.0)
    ogs = jnp.dot(spread, og_ref[...].astype(jnp.float32), preferred_element_type=jnp.float32)
    row = lax.broadcasted_iota(jnp.int32, (208, C), 0)
    og_one = jnp.where(row < 200, ogs, 0.0).astype(jnp.bfloat16)
    og_seed = jnp.where(row < 200, 0.0, ogs).astype(jnp.bfloat16)
    TN = (((0,), (0,)), ((), ()))

    def grads(pair, put):
        cols = pl.ds(pl.multiple_of(pair * WIDE, WIDE), WIDE)
        pre = jnp.dot(xs[...], ws1[:, cols], preferred_element_type=jnp.float32) + jnp.dot(
            ms[...], wn1[:, cols], preferred_element_type=jnp.float32)
        s = 1.0 / (1.0 + jnp.exp(-pre))
        h = (pre * s).astype(jnp.bfloat16)
        d = jnp.dot(og_one, wn2[:, cols], preferred_element_type=jnp.float32) / F1 + jnp.dot(
            og_seed, ws2[:, cols], preferred_element_type=jnp.float32)
        g = (d * (s * (1.0 + pre * (1.0 - s)))).astype(jnp.bfloat16)
        put(0, 768, lax.dot_general(xs[...], g, TN, preferred_element_type=jnp.float32))
        put(768, 768, lax.dot_general(ms[...], g, TN, preferred_element_type=jnp.float32))
        put(GS2, C, lax.dot_general(og_seed, h, TN, preferred_element_type=jnp.float32))
        put(GN2, C, lax.dot_general(og_one, h, TN, preferred_element_type=jnp.float32) / F1)

    core_sem = [new(), new()]
    for part in range(2):
        sib[part, :, GS2:, :] = jnp.zeros((2, ROWS_G - GS2, 128), jnp.bfloat16)

        def put(lo, n, v):
            for c in range(2):
                sib[part, c, lo:lo + n, :] = v[:, 128 * c:128 * c + 128].astype(jnp.bfloat16)
        grads((1 - core) * 2 + part, put)
        send(core_sem[part], sib.at[part], crecv.at[part], "c", 1)

    def fold(part, row0, n, srcs):
        step = min(n, 64)

        def body(k, _):
            o = pl.multiple_of(k * step, 16)
            for c in range(2):
                where = pl.ds(pl.multiple_of(row0 + o, 16), step)
                mine = pl.ds(pl.multiple_of(acc_row(part, c, row0 + o), 16), step)
                v = t32[mine, :]
                for ref in srcs:
                    v = v + ref[c, pl.ds(o, step), :].astype(jnp.float32)
                t32[mine, :] = v
                sb[part, c, where, :] = v.astype(jnp.bfloat16)
            return 0
        lax.fori_loop(0, n // step, body, 0)

    def rows(ref, part, row0, n):
        return ref.at[part, :, pl.ds(pl.multiple_of(row0, 16), n)]

    class Ring:
        def __init__(self, part, axis, base, n, buf):
            self.part, self.axis, self.base, self.n, self.buf = part, axis, base, n, buf
            self.i = {"x": x, "y": y}[axis]
            self.sem = [new() for _ in range(6)]

        def q(self, k):
            return self.base + self.n * ((self.i + k) % 4)

        def go(self, m, row0, d):
            send(self.sem[m], rows(sb, self.part, row0, self.n // 2), self.buf.at[self.part, m], self.axis, d)

        def first(self):
            h = self.n // 2
            self.go(0, self.q(2), 1)
            self.go(2, self.q(2) + h, -1)
            self.go(1, self.q(1) + h, 1)
            self.go(3, self.q(3), -1)

        def second(self):
            h = self.n // 2
            for m, row0, d in ((0, self.q(1), 1), (2, self.q(3) + h, -1)):
                arrive(self.sem[m], self.buf.at[self.part, m])
                fold(self.part, row0, h, [self.buf.at[self.part, m]])
                self.go(4 + m // 2, row0, d)

        def last(self):
            h = self.n // 2
            for m in (3, 4, 1, 5):
                arrive(self.sem[m], self.buf.at[self.part, m])
            fold(self.part, self.q(0), h, [self.buf.at[self.part, 3], self.buf.at[self.part, 4]])
            fold(self.part, self.q(0) + h, h, [self.buf.at[self.part, 1], self.buf.at[self.part, 5]])

    axes = (("x", "y"), ("y", "x"))
    rings1 = []
    for part in range(2):
        for c in range(2):
            t32[acc_row(part, c, GS2):acc_row(part, c, ROWS_G), :] = jnp.zeros((ROWS_G - GS2, 128), jnp.float32)

        def put(lo, n, v):
            for c in range(2):
                t32[acc_row(part, c, lo):acc_row(part, c, lo) + n, :] = v[:, 128 * c:128 * c + 128]
        grads(core * 2 + part, put)
        arrive(core_sem[part], crecv.at[part])
        fold(part, 0, ROWS_G, [crecv.at[part]])
        ring = Ring(part, axes[part][0], 0, 512, big)
        ring.first()
        rings1.append(ring)
    for ring in rings1:
        ring.second()
    rings2 = []
    for ring in rings1:
        ring.last()
        nxt = Ring(ring.part, axes[ring.part][1], ring.q(0), 128, small)
        nxt.first()
        rings2.append(nxt)
    for ring in rings2:
        ring.second()
    zsem = [[new() for _ in range(NZ - 1)] for _ in range(2)]
    for ring in rings2:
        ring.last()
        for k in range(1, NZ):
            send(zsem[ring.part][k - 1], rows(sb, ring.part, ring.q(0) + 16 * ((z + k) % NZ), 16), tiny.at[ring.part, k - 1], "z", k)

    def final(part, row0, n):
        return fin.at[pl.ds(4 * core + 2 * part, 2), pl.ds(pl.multiple_of(row0, 16), n)]

    fsem = [[new() for _ in range(NZ - 1)] for _ in range(2)]
    for ring in rings2:
        p = ring.part
        for k in range(1, NZ):
            arrive(zsem[p][k - 1], tiny.at[p, k - 1])
        r0 = pl.multiple_of(ring.q(0) + 16 * z, 16)
        for c in range(2):
            v = t32[pl.ds(pl.multiple_of(acc_row(p, c, r0), 16), 16), :]
            for k in range(NZ - 1):
                v = v + tiny[p, k, c].astype(jnp.float32)
            fin[4 * core + 2 * p + c, pl.ds(r0, 16), :] = v.astype(jnp.bfloat16)
        for k in range(1, NZ):
            here = final(p, r0, 16)
            send(fsem[p][k - 1], here, here, "z", k)

    def spread_first(part, axis, base, n, i, sem):
        here = final(part, base + n * i, n)
        send(sem[0], here, here, axis, 1)
        send(sem[1], here, here, axis, -1)

    def spread_second(part, axis, base, n, i, sem):
        h = n // 2
        a = base + n * ((i + 3) % 4)
        arrive(sem[0], final(part, a, n))
        here = final(part, a, h)
        send(sem[2], here, here, axis, 1)
        b = base + n * ((i + 1) % 4)
        arrive(sem[1], final(part, b, n))
        here = final(part, b + h, h)
        send(sem[3], here, here, axis, -1)
        return a, b

    def spread_last(part, axis, base, n, i, sem):
        o = base + n * ((i + 2) % 4)
        arrive(sem[2], final(part, o, n // 2))
        arrive(sem[3], final(part, o + n // 2, n // 2))
        return o

    sems = [[new() for _ in range(4)] for _ in range(2)]
    for ring in rings2:
        for k in range(1, NZ):
            arrive(fsem[ring.part][k - 1], final(ring.part, ring.q(0) + 16 * ((z - k + NZ) % NZ), 16))
        spread_first(ring.part, ring.axis, ring.base, 128, ring.i, sems[ring.part])
    for ring in rings2:
        spread_second(ring.part, ring.axis, ring.base, 128, ring.i, sems[ring.part])
    sems1 = [[new() for _ in range(4)] for _ in range(2)]
    csem = [[new() for _ in range(4)] for _ in range(2)]

    def across(part, k, row0):
        here = final(part, row0, 512)
        send(csem[part][k], here, here, "c", 1)

    for ring in rings2:
        p = ring.part
        spread_last(p, ring.axis, ring.base, 128, ring.i, sems[p])
        spread_first(p, axes[p][0], 0, 512, rings1[p].i, sems1[p])
        across(p, 0, rings1[p].q(0))
    for ring in rings1:
        p = ring.part
        a, b = spread_second(p, ring.axis, 0, 512, ring.i, sems1[p])
        across(p, 1, a)
        across(p, 2, b)
    for ring in rings1:
        p = ring.part
        across(p, 3, spread_last(p, ring.axis, 0, 512, ring.i, sems1[p]))
    for ring in rings1:
        p = ring.part
        for k, off in enumerate((0, 3, 1, 2)):
            here = fin.at[pl.ds(4 * (1 - core) + 2 * p, 2), pl.ds(pl.multiple_of(ring.q(off), 16), 512)]
            arrive(csem[p][k], here)
    outs = []
    for h in range(8):
        for n, (ref, lo) in enumerate(((gs1, 0), (gn1, 768))):
            outs.append(pltpu.make_async_copy(fin.at[h, pl.ds(lo, 768)], ref.at[:, pl.ds(128 * h, 128)], lsem.at[4 + 2 * h + n]))
            outs[-1].start()
    for h in range(8):
        for ref, lo in ((gs2, GS2), (gn2, GN2)):
            ref[:, 128 * h:128 * h + 128] = fin[h, lo:lo + C, :]
    for c in outs:
        c.wait()
    for c in sent:
        c.wait_send()
    for k in range(1, REP):
        ocopy(k).wait_send()
        icopy(k).wait_send()
    for i, m in enumerate(PLAN):
        ag_copy(m, i).wait_send()
    assert counter[0] == N_SEM, counter[0]


def per_device(
    table, near_owner, near_row, far_owner, far_row, w_self1, w_neigh1, w_self2, w_neigh2, out_grad
):
    bf, f32, n = jnp.bfloat16, jnp.float32, len(PLAN)
    vmem, hbm, dma = pl.BlockSpec(memory_space=pltpu.VMEM), pl.BlockSpec(memory_space=pl.ANY), pltpu.SemaphoreType.DMA
    turned = [w_self2.T, w_neigh2.T]
    out = pl.pallas_call(
        kernel,
        out_shape=[jax.ShapeDtypeStruct(a.shape, bf) for a in (w_self1, w_neigh1, *turned)],
        in_specs=[vmem] * 4 + [hbm] * 3 + [vmem] * 3,
        out_specs=[hbm, hbm, vmem, vmem],
        scratch_shapes=[
            pltpu.VMEM((ROWS, 256), bf),
            pltpu.VMEM((NZ * NX, G4, 384), bf),
            pltpu.VMEM((NZ * NX * ROWS, 128), f32),
            pltpu.VMEM((208, 128), f32),
            pltpu.VMEM((208, 128), f32),
            pltpu.VMEM((REP, 416, 128), bf),
            pltpu.VMEM((REP, 416, 128), bf),
            pltpu.VMEM((GROUPS, 8, 128), jnp.int32),
            pltpu.VMEM((REP, GROUPS, 8, 128), jnp.int32),
            pltpu.SMEM((REP, GROUPS, 8, 128), jnp.int32),
            pltpu.VMEM((768, 1024), bf),
            pltpu.VMEM((768, 1024), bf),
            pltpu.VMEM((208, 768), bf),
            pltpu.VMEM((208, 768), bf),
            pltpu.VMEM((2, 2, ROWS_G, 128), bf),
            pltpu.VMEM((2, 2, ROWS_G, 128), bf),
            pltpu.VMEM((2, 2, ROWS_G, 128), bf),
            pltpu.VMEM((2, 6, 2, 256, 128), bf),
            pltpu.VMEM((2, 6, 2, 64, 128), bf),
            pltpu.VMEM((2, 7, 2, 16, 128), bf),
            pltpu.VMEM((8, ROWS_G, 128), bf),
            dma((n,)), dma((n,)), dma((REP,)), dma((REP,)), dma((REP,)), dma((REP,)), dma((N_SEM,)), dma((N_SEM,)), dma((20,)),
        ],
        compiler_params=pltpu.CompilerParams(collective_id=0, has_side_effects=True, vmem_limit_bytes=61 * 10**6),
        cost_estimate=pl.CostEstimate(flops=4 * 10**9, bytes_accessed=3 * 10**7, transcendentals=0),
        name="step",
    )(near_owner.reshape(near_row.shape), near_row, far_owner.reshape(far_row.shape), far_row, table,
      w_self1, w_neigh1, *turned, out_grad)
    return out[0], out[1], out[2].T, out[3].T


def solution(mesh):
    rows = P(("node", "rep"))
    return jax.shard_map(
        per_device,
        mesh=mesh,
        in_specs=(P("node"), rows, rows, rows, rows, P(), P(), P(), P(), rows),
        out_specs=(P(), P(), P(), P()),
        check_vma=False,
    )
```

```python
import jax
import jax.numpy as jnp
from jax import lax
from jax.experimental import pallas as pl
from jax.experimental.pallas import tpu as pltpu
from jax.sharding import PartitionSpec as P

MESH = pl.DeviceIdType.MESH
NZ, NX, REP = 8, 4, 8
ROWS, W = 1536, 96
F1, F2 = 25, 15
G4 = ROWS // 4
UNITS = ((0, 80), (80, 80), (160, 112), (272, 112))
WIDE = 256
ROWS_G = 2048
C = 153
GS2, GN2 = 1536, 1696
PARTS = 4
N_SEM = PARTS * (1 + 6 + 6 + 7 + 7 + 4 + 4 + 4)
GROUPS = 5


def plan():
    msgs = []
    def hops(size, half):
        out = []
        for h in range(1, size // 2 + 1):
            for d in (1, -1):
                if 2 * h == size and (d == 1) != (half == 0):
                    continue
                out.append((h, d))
        return out
    for u in range(4):
        half = u % 2
        first, second = ("x", "z") if u < 2 else ("z", "x")
        size = {"x": NX, "z": NZ}
        reach = [(0, 0)]
        for h, d in hops(size[first], half):
            off = {first: -h * d, second: 0}
            msgs.append((h, u, off["x"], off["z"], first, d))
            reach.append((-h * d, h))
        for o, base in reach:
            for h, d in hops(size[second], half):
                off = {first: o, second: -h * d}
                msgs.append((base + h, u, off["x"], off["z"], second, d))
    msgs.sort(key=lambda m: m[0])
    return msgs


PLAN = plan()


def kernel(no_ref, nr_ref, fo_ref, fr_ref, table, ws1_h, wn1_h, ws2, wn2, og_ref, gs1, gn1, gs2, gn2,
           tw, land, t32, sums, ones, stage, got, idx_own, idx_land, idx_smem, ws1, wn1,
           xs, ms, sb, sib, crecv, big, small, tiny, fin,
           ag_send, ag_recv, isend, irecv, osend, orecv, send_sem, recv_sem, lsem):
    node, rep = lax.axis_index("node"), lax.axis_index("rep")
    z, x = node // NX, node % NX
    y, core = rep // 2, rep % 2
    window = pl.multiple_of(128 * jnp.minimum(3 * rep // 4, 4), 128)
    get_table = pltpu.make_async_copy(table.at[:, pl.ds(window, 256)], tw, lsem.at[0])
    get_table.start()
    get_ws1 = pltpu.make_async_copy(ws1_h, ws1, lsem.at[1])
    get_wn1 = pltpu.make_async_copy(wn1_h, wn1, lsem.at[2])
    get_ws1.start()
    get_wn1.start()

    def at(dx, dz):
        return ((z + dz + 2 * NZ) % NZ) * NX + (x + dx + 2 * NX) % NX

    def dev(axis, d):
        if axis == "x":
            return (at(d, 0), rep)
        if axis == "y":
            return (node, ((y + d + 4) % 4) * 2 + core)
        if axis == "z":
            return (at(0, d), rep)
        if axis == "rep":
            return (node, (rep + d) % REP)
        return (node, y * 2 + 1 - core)

    barrier = pltpu.get_barrier_semaphore()
    peers = [("x", 1), ("x", -1)] + [("z", k) for k in range(1, NZ)] + [("rep", k) for k in range(1, REP)]
    for axis, d in peers:
        pl.semaphore_signal(barrier, inc=1, device_id=dev(axis, d), device_id_type=MESH)

    far = fo_ref[...] * ROWS + fr_ref[...]
    near = no_ref[...] * ROWS + nr_ref[...]
    idx_own[...] = jnp.zeros_like(idx_own)
    for t in range(GROUPS):
        idx_own[t, :, 0:75] = far[:, 75 * t:75 * t + 75]
        idx_own[t, :, 75:80] = near[:, 1 + 5 * t:6 + 5 * t]
        idx_own[t, :, 80:81] = near[:, 0:1]

    c = lax.broadcasted_iota(jnp.int32, (256, 384), 0)
    d = lax.broadcasted_iota(jnp.int32, (256, 384), 1)
    j = d // 128
    hit = c == rep * W - window + j * 32 + d % 32
    group = jnp.where(hit, ((d // 32) % 4 - j + 4) % 4, -1)
    perms = [jnp.where(group == g, 1.0, 0.0).astype(jnp.bfloat16) for g in range(4)]
    get_table.wait()

    def pack(lo, n):
        acc = jnp.zeros((n, 384), jnp.float32)
        for g in range(4):
            acc = acc + jnp.dot(tw[g * G4 + lo:g * G4 + lo + n, :], perms[g], preferred_element_type=jnp.float32)
        land[node, lo:lo + n, :] = acc.astype(jnp.bfloat16)

    def slot(u, n):
        return land.at[n, pl.ds(UNITS[u][0], UNITS[u][1])]

    def ag_copy(m, i):
        _, u, ox, oz, axis, dr = m
        s = slot(u, at(ox + dr, oz) if axis == "x" else at(ox, oz + dr))
        return pltpu.make_async_remote_copy(src_ref=s, dst_ref=s, send_sem=ag_send.at[i], recv_sem=ag_recv.at[i],
                                            device_id=dev(axis, dr), device_id_type=MESH)

    def ag_arrival(m, i):
        s = slot(m[1], at(m[2], m[3]))
        return pltpu.make_async_remote_copy(src_ref=s, dst_ref=s, send_sem=ag_send.at[i], recv_sem=ag_recv.at[i],
                                            device_id=dev("rep", 1), device_id_type=MESH)

    lane = lax.broadcasted_iota(jnp.int32, (96, 128), 1) // 32

    def unpack(n, half):
        def body(i, _):
            r0 = pl.multiple_of(i * 96, 16)
            p = land[n, pl.ds(r0, 96), :].astype(jnp.float32)
            ps = [p[:, 128 * q:128 * q + 128] for q in range(3)]
            for g in range(4):
                s = jnp.where(lane == g, ps[0], jnp.where(lane == (g + 1) % 4, ps[1], jnp.where(lane == (g + 2) % 4, ps[2], 0.0)))
                if g:
                    s = pltpu.roll(s, 128 - 32 * g, 1)
                t32[pl.ds(pl.multiple_of(n * ROWS + g * G4 + r0, 16), 96), :] = s
            return 0
        lax.fori_loop(2 * half, 2 * half + 2, body, 0)

    started = set()

    def start_children(u, ox, oz):
        for i, m in enumerate(PLAN):
            if m[1] != u or i in started:
                continue
            sx, sz = (m[2] + m[5], m[3]) if m[4] == "x" else (m[2], m[3] + m[5])
            if (sx % NX, sz % NZ) == (ox % NX, oz % NZ):
                started.add(i)
                ag_copy(m, i).start()

    pack(0, 160)
    pl.semaphore_wait(barrier, len(peers))
    for u in (0, 1):
        start_children(u, 0, 0)
    pack(160, 224)
    for u in (2, 3):
        start_children(u, 0, 0)

    def icopy(k):
        return pltpu.make_async_remote_copy(src_ref=idx_own, dst_ref=idx_land.at[rep], send_sem=isend.at[k], recv_sem=irecv.at[k],
                                            device_id=dev("rep", k), device_id_type=MESH)
    for k in range(1, REP):
        icopy(k).start()
    idx_land[rep] = idx_own[...]
    work = [(0, 0, 0), (0, 0, 1)]
    for t in range(1, PLAN[-1][0] + 1):
        seen = []
        for i, m in enumerate(PLAN):
            if m[0] != t:
                continue
            ag_arrival(m, i).wait_recv()
            start_children(m[1], m[2], m[3])
            if (m[2] % NX, m[3] % NZ) not in seen:
                seen.append((m[2] % NX, m[3] % NZ))
            if work:
                ox, oz, half = work.pop(0)
                unpack(at(ox, oz), half)
        work += [(ox, oz, half) for ox, oz in seen for half in range(2)]
        if t == 2:
            for k in range(1, REP):
                icopy(k).wait_recv()
            to_smem = pltpu.make_async_copy(idx_land, idx_smem, lsem.at[3])
            to_smem.start()
    for ox, oz, half in work:
        unpack(at(ox, oz), half)
    to_smem.wait()

    def ocopy(k):
        return pltpu.make_async_remote_copy(src_ref=stage.at[k], dst_ref=got.at[rep], send_sem=osend.at[k], recv_sem=orecv.at[k],
                                            device_id=dev("rep", k), device_id_type=MESH)

    def arrived_slice(k):
        there = got.at[(rep - k + REP) % REP]
        return pltpu.make_async_remote_copy(src_ref=there, dst_ref=there, send_sem=osend.at[k], recv_sem=orecv.at[k],
                                            device_id=dev("rep", k), device_id_type=MESH)

    sums[200:208, :] = jnp.zeros((8, 128), jnp.float32)
    for k in list(range(1, REP)) + [0]:
        p = (rep + k) % REP

        def body(i, _):
            t = i // 4
            for half in range(2):
                b = i % 4 * 2 + half

                def row(q):
                    return t32[pl.ds(idx_smem[p, t, b, q], 1), :]
                for u in range(5):
                    rows = [row(u * F2 + q) for q in range(F2)]
                    while len(rows) > 1:
                        rows = [rows[a] + rows[a + 1] if a + 1 < len(rows) else rows[a] for a in range(0, len(rows), 2)]
                    sums[pl.ds(b * F1 + t * 5 + u, 1), :] = rows[0]
                    ones[pl.ds(b * F1 + t * 5 + u, 1), :] = row(75 + u)
            return 0
        lax.fori_loop(0, 4 * GROUPS, body, 0)
        for b in range(8):
            ones[pl.ds(200 + b, 1), :] = t32[pl.ds(idx_smem[p, 0, b, 80], 1), :]
        for h, part in ((0, sums[...] / F2), (1, ones[...])):
            if k:
                stage[k, 208 * h:208 * h + 208, :] = part.astype(jnp.bfloat16)
            else:
                got[rep, 208 * h:208 * h + 208, :] = part.astype(jnp.bfloat16)
        if k:
            ocopy(k).start()
    get_ws1.wait()
    get_wn1.wait()
    for k in range(1, REP):
        arrived_slice(k).wait_recv()
    counter = [0]

    def acc_row(part, row):
        return part * ROWS_G + row

    def new():
        counter[0] += 1
        return counter[0] - 1

    def copy(i, src, dst, axis, d):
        return pltpu.make_async_remote_copy(src_ref=src, dst_ref=dst, send_sem=send_sem.at[i], recv_sem=recv_sem.at[i],
                                            device_id=dev(axis, d), device_id_type=MESH)
    sent = []

    def send(i, src, dst, axis, d):
        c = copy(i, src, dst, axis, d)
        c.start()
        sent.append(c)

    def arrive(i, dst):
        copy(i, dst, dst, "c", 1).wait_recv()

    for ref, lo in ((ms, 0), (xs, 208)):
        lane = lax.broadcasted_iota(jnp.int32, (208, 128), 1)
        chunks = [None] * 6
        for r in range(REP):
            q, o = 96 * r // 128, 96 * r % 128
            v = got[r, lo:lo + 208, :].astype(jnp.float32)
            if o:
                v = pltpu.roll(v, o, 1)
            here = jnp.where(lane >= o, v, 0.0) if o > 32 else v
            chunks[q] = here if chunks[q] is None else chunks[q] + here
            if o > 32:
                chunks[q + 1] = jnp.where(lane < o, v, 0.0)
        for q in range(6):
            ref[:, 128 * q:128 * q + 128] = chunks[q].astype(jnp.bfloat16)
    r8 = lax.broadcasted_iota(jnp.int32, (8, 208), 0)
    c8 = lax.broadcasted_iota(jnp.int32, (8, 208), 1)
    pick = jnp.where((c8 < 200) & (c8 // F1 == r8), 1.0, 0.0).astype(jnp.bfloat16)
    mean_one = jnp.dot(pick, xs[...], preferred_element_type=jnp.float32) / F1
    ms[192:208, :] = jnp.concatenate([ms[192:208, :].astype(jnp.float32)[:8], mean_one], axis=0).astype(jnp.bfloat16)
    rr = lax.broadcasted_iota(jnp.int32, (208, 8), 0)
    cc = lax.broadcasted_iota(jnp.int32, (208, 8), 1)
    spread = jnp.where(jnp.where(rr < 200, rr // F1, rr - 200) == cc, 1.0, 0.0)
    ogs = jnp.dot(spread, og_ref[...].astype(jnp.float32), preferred_element_type=jnp.float32)
    row = lax.broadcasted_iota(jnp.int32, (208, C), 0)
    og_one = jnp.where(row < 200, ogs, 0.0).astype(jnp.bfloat16)
    og_seed = jnp.where(row < 200, 0.0, ogs).astype(jnp.bfloat16)
    TN = (((0,), (0,)), ((), ()))

    def grads(pair, put):
        cols = pl.ds(pl.multiple_of(pair * WIDE, WIDE), WIDE)
        pre = jnp.dot(xs[...], ws1[:, cols], preferred_element_type=jnp.float32) + jnp.dot(
            ms[...], wn1[:, cols], preferred_element_type=jnp.float32)
        s = 1.0 / (1.0 + jnp.exp(-pre))
        h = (pre * s).astype(jnp.bfloat16)
        d = jnp.dot(og_one, wn2[:, cols], preferred_element_type=jnp.float32) / F1 + jnp.dot(
            og_seed, ws2[:, cols], preferred_element_type=jnp.float32)
        g = (d * (s * (1.0 + pre * (1.0 - s)))).astype(jnp.bfloat16)
        put(0, 768, lax.dot_general(xs[...], g, TN, preferred_element_type=jnp.float32))
        put(768, 768, lax.dot_general(ms[...], g, TN, preferred_element_type=jnp.float32))
        put(GS2, C, lax.dot_general(og_seed, h, TN, preferred_element_type=jnp.float32))
        put(GN2, C, lax.dot_general(og_one, h, TN, preferred_element_type=jnp.float32) / F1)

    core_sem = [new() for _ in range(PARTS)]
    for pair in range(2):
        parts = (2 * pair, 2 * pair + 1)
        sib[2 * pair:2 * pair + 2, GS2:, :] = jnp.zeros((2, ROWS_G - GS2, 128), jnp.bfloat16)

        def put(lo, n, v):
            for c in range(2):
                sib[parts[c], lo:lo + n, :] = v[:, 128 * c:128 * c + 128].astype(jnp.bfloat16)
        grads((1 - core) * 2 + pair, put)
        for p in parts:
            send(core_sem[p], sib.at[p], crecv.at[p], "c", 1)

    def fold(part, row0, n, srcs):
        step = min(n, 128)

        def body(k, _):
            o = pl.multiple_of(k * step, 16)
            mine = pl.ds(pl.multiple_of(acc_row(part, row0 + o), 16), step)
            v = t32[mine, :]
            for ref in srcs:
                v = v + ref[pl.ds(o, step), :].astype(jnp.float32)
            t32[mine, :] = v
            sb[part, pl.ds(pl.multiple_of(row0 + o, 16), step), :] = v.astype(jnp.bfloat16)
            return 0
        lax.fori_loop(0, n // step, body, 0)

    def rows(ref, part, row0, n):
        return ref.at[part, pl.ds(pl.multiple_of(row0, 16), n)]

    class Ring:
        def __init__(self, part, axis, base, n, buf):
            self.part, self.axis, self.base, self.n, self.buf = part, axis, base, n, buf
            self.i = {"x": x, "y": y}[axis]
            self.sem = [new() for _ in range(6)]

        def q(self, k):
            return self.base + self.n * ((self.i + k) % 4)

        def go(self, m, row0, d):
            send(self.sem[m], rows(sb, self.part, row0, self.n // 2), self.buf.at[self.part, m], self.axis, d)

        def first(self):
            h = self.n // 2
            self.go(0, self.q(2), 1)
            self.go(2, self.q(2) + h, -1)
            self.go(1, self.q(1) + h, 1)
            self.go(3, self.q(3), -1)

        def second(self):
            h = self.n // 2
            for m, row0, d in ((0, self.q(1), 1), (2, self.q(3) + h, -1)):
                arrive(self.sem[m], self.buf.at[self.part, m])
                fold(self.part, row0, h, [self.buf.at[self.part, m]])
                self.go(4 + m // 2, row0, d)

        def last(self):
            h = self.n // 2
            for m in (3, 4, 1, 5):
                arrive(self.sem[m], self.buf.at[self.part, m])
            fold(self.part, self.q(0), h, [self.buf.at[self.part, 3], self.buf.at[self.part, 4]])
            fold(self.part, self.q(0) + h, h, [self.buf.at[self.part, 1], self.buf.at[self.part, 5]])

    axes = (("x", "y"), ("y", "x")) * (PARTS // 2)
    rings1 = []
    for pair in range(2):
        parts = (2 * pair, 2 * pair + 1)
        for p in parts:
            t32[acc_row(p, GS2):acc_row(p, ROWS_G), :] = jnp.zeros((ROWS_G - GS2, 128), jnp.float32)

        def put(lo, n, v):
            for c in range(2):
                t32[acc_row(parts[c], lo):acc_row(parts[c], lo) + n, :] = v[:, 128 * c:128 * c + 128]
        grads(core * 2 + pair, put)
        for p in parts:
            arrive(core_sem[p], crecv.at[p])
            fold(p, 0, ROWS_G, [crecv.at[p]])
            ring = Ring(p, axes[p][0], 0, 512, big)
            ring.first()
            rings1.append(ring)
    for ring in rings1:
        ring.second()
    rings2 = []
    for ring in rings1:
        ring.last()
        nxt = Ring(ring.part, axes[ring.part][1], ring.q(0), 128, small)
        nxt.first()
        rings2.append(nxt)
    for ring in rings2:
        ring.second()
    zsem = [[new() for _ in range(NZ - 1)] for _ in range(PARTS)]
    for ring in rings2:
        ring.last()
        for k in range(1, NZ):
            send(zsem[ring.part][k - 1], rows(sb, ring.part, ring.q(0) + 16 * ((z + k) % NZ), 16), tiny.at[ring.part, k - 1], "z", k)

    def final(part, row0, n):
        return fin.at[4 * core + part, pl.ds(pl.multiple_of(row0, 16), n)]

    fsem = [[new() for _ in range(NZ - 1)] for _ in range(PARTS)]
    for ring in rings2:
        p = ring.part
        for k in range(1, NZ):
            arrive(zsem[p][k - 1], tiny.at[p, k - 1])
        r0 = pl.multiple_of(ring.q(0) + 16 * z, 16)
        v = t32[pl.ds(pl.multiple_of(acc_row(p, r0), 16), 16), :]
        for k in range(NZ - 1):
            v = v + tiny[p, k].astype(jnp.float32)
        fin[4 * core + p, pl.ds(r0, 16), :] = v.astype(jnp.bfloat16)
        for k in range(1, NZ):
            here = final(p, r0, 16)
            send(fsem[p][k - 1], here, here, "z", k)

    def spread_first(part, axis, base, n, i, sem):
        here = final(part, base + n * i, n)
        send(sem[0], here, here, axis, 1)
        send(sem[1], here, here, axis, -1)

    def spread_second(part, axis, base, n, i, sem):
        h = n // 2
        a = base + n * ((i + 3) % 4)
        arrive(sem[0], final(part, a, n))
        here = final(part, a, h)
        send(sem[2], here, here, axis, 1)
        b = base + n * ((i + 1) % 4)
        arrive(sem[1], final(part, b, n))
        here = final(part, b + h, h)
        send(sem[3], here, here, axis, -1)
        return a, b

    def spread_last(part, axis, base, n, i, sem):
        o = base + n * ((i + 2) % 4)
        arrive(sem[2], final(part, o, n // 2))
        arrive(sem[3], final(part, o + n // 2, n // 2))
        return o

    sems = [[new() for _ in range(4)] for _ in range(PARTS)]
    for ring in rings2:
        for k in range(1, NZ):
            arrive(fsem[ring.part][k - 1], final(ring.part, ring.q(0) + 16 * ((z - k + NZ) % NZ), 16))
        spread_first(ring.part, ring.axis, ring.base, 128, ring.i, sems[ring.part])
    for ring in rings2:
        spread_second(ring.part, ring.axis, ring.base, 128, ring.i, sems[ring.part])
    sems1 = [[new() for _ in range(4)] for _ in range(PARTS)]
    csem = [[new() for _ in range(4)] for _ in range(PARTS)]

    def across(part, k, row0):
        here = final(part, row0, 512)
        send(csem[part][k], here, here, "c", 1)

    for ring in rings2:
        p = ring.part
        spread_last(p, ring.axis, ring.base, 128, ring.i, sems[p])
        spread_first(p, axes[p][0], 0, 512, rings1[p].i, sems1[p])
        across(p, 0, rings1[p].q(0))
    for ring in rings1:
        p = ring.part
        a, b = spread_second(p, ring.axis, 0, 512, ring.i, sems1[p])
        across(p, 1, a)
        across(p, 2, b)
    for ring in rings1:
        p = ring.part
        across(p, 3, spread_last(p, ring.axis, 0, 512, ring.i, sems1[p]))
    for ring in rings1:
        p = ring.part
        for k, off in enumerate((0, 3, 1, 2)):
            here = fin.at[4 * (1 - core) + p, pl.ds(pl.multiple_of(ring.q(off), 16), 512)]
            arrive(csem[p][k], here)
    outs = []
    for h in range(8):
        for n, (ref, lo) in enumerate(((gs1, 0), (gn1, 768))):
            outs.append(pltpu.make_async_copy(fin.at[h, pl.ds(lo, 768)], ref.at[:, pl.ds(128 * h, 128)], lsem.at[4 + 2 * h + n]))
            outs[-1].start()
    for h in range(8):
        for ref, lo in ((gs2, GS2), (gn2, GN2)):
            ref[:, 128 * h:128 * h + 128] = fin[h, lo:lo + C, :]
    for c in outs:
        c.wait()
    for c in sent:
        c.wait_send()
    for k in range(1, REP):
        ocopy(k).wait_send()
        icopy(k).wait_send()
    for i, m in enumerate(PLAN):
        ag_copy(m, i).wait_send()
    assert counter[0] == N_SEM, counter[0]


def per_device(
    table, near_owner, near_row, far_owner, far_row, w_self1, w_neigh1, w_self2, w_neigh2, out_grad
):
    bf, f32, n = jnp.bfloat16, jnp.float32, len(PLAN)
    vmem, hbm, dma = pl.BlockSpec(memory_space=pltpu.VMEM), pl.BlockSpec(memory_space=pl.ANY), pltpu.SemaphoreType.DMA
    turned = [w_self2.T, w_neigh2.T]
    out = pl.pallas_call(
        kernel,
        out_shape=[jax.ShapeDtypeStruct(a.shape, bf) for a in (w_self1, w_neigh1, *turned)],
        in_specs=[vmem] * 4 + [hbm] * 3 + [vmem] * 3,
        out_specs=[hbm, hbm, vmem, vmem],
        scratch_shapes=[
            pltpu.VMEM((ROWS, 256), bf),
            pltpu.VMEM((NZ * NX, G4, 384), bf),
            pltpu.VMEM((NZ * NX * ROWS, 128), f32),
            pltpu.VMEM((208, 128), f32),
            pltpu.VMEM((208, 128), f32),
            pltpu.VMEM((REP, 416, 128), bf),
            pltpu.VMEM((REP, 416, 128), bf),
            pltpu.VMEM((GROUPS, 8, 128), jnp.int32),
            pltpu.VMEM((REP, GROUPS, 8, 128), jnp.int32),
            pltpu.SMEM((REP, GROUPS, 8, 128), jnp.int32),
            pltpu.VMEM((768, 1024), bf),
            pltpu.VMEM((768, 1024), bf),
            pltpu.VMEM((208, 768), bf),
            pltpu.VMEM((208, 768), bf),
            pltpu.VMEM((PARTS, ROWS_G, 128), bf),
            pltpu.VMEM((PARTS, ROWS_G, 128), bf),
            pltpu.VMEM((PARTS, ROWS_G, 128), bf),
            pltpu.VMEM((PARTS, 6, 256, 128), bf),
            pltpu.VMEM((PARTS, 6, 64, 128), bf),
            pltpu.VMEM((PARTS, 7, 16, 128), bf),
            pltpu.VMEM((8, ROWS_G, 128), bf),
            dma((n,)), dma((n,)), dma((REP,)), dma((REP,)), dma((REP,)), dma((REP,)), dma((N_SEM,)), dma((N_SEM,)), dma((20,)),
        ],
        compiler_params=pltpu.CompilerParams(collective_id=0, has_side_effects=True, vmem_limit_bytes=61 * 10**6),
        cost_estimate=pl.CostEstimate(flops=4 * 10**9, bytes_accessed=3 * 10**7, transcendentals=0),
        name="step",
    )(near_owner.reshape(near_row.shape), near_row, far_owner.reshape(far_row.shape), far_row, table,
      w_self1, w_neigh1, *turned, out_grad)
    return out[0], out[1], out[2].T, out[3].T


def solution(mesh):
    rows = P(("node", "rep"))
    return jax.shard_map(
        per_device,
        mesh=mesh,
        in_specs=(P("node"), rows, rows, rows, rows, P(), P(), P(), P(), rows),
        out_specs=(P(), P(), P(), P()),
        check_vma=False,
    )
```

```python
import jax
import jax.numpy as jnp
from jax import lax
from jax.experimental import pallas as pl
from jax.experimental.pallas import tpu as pltpu
from jax.sharding import PartitionSpec as P

MESH = pl.DeviceIdType.MESH
NZ, NX, REP = 8, 4, 8
ROWS, W = 1536, 96
F1, F2 = 25, 15
G4 = ROWS // 4
UNITS = ((0, 80), (80, 80), (160, 112), (272, 112))
WIDE = 256
ROWS_G = 2048
C = 153
GS2, GN2 = 1536, 1696
PARTS = 4
N_SEM = PARTS * (1 + 6 + 6 + 7 + 7 + 4 + 4 + 4)
GROUPS = 5


def plan():
    msgs = []
    def hops(size, half):
        out = []
        for h in range(1, size // 2 + 1):
            for d in (1, -1):
                if 2 * h == size and (d == 1) != (half == 0):
                    continue
                out.append((h, d))
        return out
    for u in range(4):
        half = u % 2
        first, second = ("x", "z") if u < 2 else ("z", "x")
        size = {"x": NX, "z": NZ}
        reach = [(0, 0)]
        for h, d in hops(size[first], half):
            off = {first: -h * d, second: 0}
            msgs.append((h, u, off["x"], off["z"], first, d))
            reach.append((-h * d, h))
        for o, base in reach:
            for h, d in hops(size[second], half):
                off = {first: o, second: -h * d}
                msgs.append((base + h, u, off["x"], off["z"], second, d))
    msgs.sort(key=lambda m: m[0])
    return msgs


PLAN = plan()


def kernel(no_ref, nr_ref, fo_ref, fr_ref, table, ws1_h, wn1_h, ws2, wn2, og_ref, gs1, gn1, gs2, gn2,
           tw, land, t32, sums, ones, stage, got, idx_own, idx_land, idx_smem, ws1, wn1,
           xs, ms, sb, sib, crecv, big, small, tiny, fin,
           ag_send, ag_recv, isend, irecv, osend, orecv, send_sem, recv_sem, lsem):
    node, rep = lax.axis_index("node"), lax.axis_index("rep")
    z, x = node // NX, node % NX
    y, core = rep // 2, rep % 2
    window = pl.multiple_of(128 * jnp.minimum(3 * rep // 4, 4), 128)
    get_table = pltpu.make_async_copy(table.at[:, pl.ds(window, 256)], tw, lsem.at[0])
    get_table.start()
    get_ws1 = pltpu.make_async_copy(ws1_h, ws1, lsem.at[1])
    get_wn1 = pltpu.make_async_copy(wn1_h, wn1, lsem.at[2])
    get_ws1.start()
    get_wn1.start()

    def at(dx, dz):
        return ((z + dz + 2 * NZ) % NZ) * NX + (x + dx + 2 * NX) % NX

    def dev(axis, d):
        if axis == "x":
            return (at(d, 0), rep)
        if axis == "y":
            return (node, ((y + d + 4) % 4) * 2 + core)
        if axis == "z":
            return (at(0, d), rep)
        if axis == "rep":
            return (node, (rep + d) % REP)
        return (node, y * 2 + 1 - core)

    barrier = pltpu.get_barrier_semaphore()
    peers = [("x", 1), ("x", -1)] + [("z", k) for k in range(1, NZ)] + [("rep", k) for k in range(1, REP)]
    for axis, d in peers:
        pl.semaphore_signal(barrier, inc=1, device_id=dev(axis, d), device_id_type=MESH)

    far = fo_ref[...] * ROWS + fr_ref[...]
    near = no_ref[...] * ROWS + nr_ref[...]
    idx_own[...] = jnp.zeros_like(idx_own)
    for t in range(GROUPS):
        idx_own[t, :, 0:75] = far[:, 75 * t:75 * t + 75]
        idx_own[t, :, 75:80] = near[:, 1 + 5 * t:6 + 5 * t]
        idx_own[t, :, 80:81] = near[:, 0:1]

    c = lax.broadcasted_iota(jnp.int32, (256, 384), 0)
    d = lax.broadcasted_iota(jnp.int32, (256, 384), 1)
    j = d // 128
    hit = c == rep * W - window + j * 32 + d % 32
    group = jnp.where(hit, ((d // 32) % 4 - j + 4) % 4, -1)
    perms = [jnp.where(group == g, 1.0, 0.0).astype(jnp.bfloat16) for g in range(4)]
    get_table.wait()

    def pack(lo, n):
        acc = jnp.zeros((n, 384), jnp.float32)
        for g in range(4):
            acc = acc + jnp.dot(tw[g * G4 + lo:g * G4 + lo + n, :], perms[g], preferred_element_type=jnp.float32)
        land[node, lo:lo + n, :] = acc.astype(jnp.bfloat16)

    def slot(u, n):
        return land.at[n, pl.ds(UNITS[u][0], UNITS[u][1])]

    def ag_copy(m, i):
        _, u, ox, oz, axis, dr = m
        s = slot(u, at(ox + dr, oz) if axis == "x" else at(ox, oz + dr))
        return pltpu.make_async_remote_copy(src_ref=s, dst_ref=s, send_sem=ag_send.at[i], recv_sem=ag_recv.at[i],
                                            device_id=dev(axis, dr), device_id_type=MESH)

    def ag_arrival(m, i):
        s = slot(m[1], at(m[2], m[3]))
        return pltpu.make_async_remote_copy(src_ref=s, dst_ref=s, send_sem=ag_send.at[i], recv_sem=ag_recv.at[i],
                                            device_id=dev("rep", 1), device_id_type=MESH)

    lane = lax.broadcasted_iota(jnp.int32, (96, 128), 1) // 32

    def unpack(n, half):
        def body(i, _):
            r0 = pl.multiple_of(i * 96, 16)
            p = land[n, pl.ds(r0, 96), :].astype(jnp.float32)
            ps = [p[:, 128 * q:128 * q + 128] for q in range(3)]
            for g in range(4):
                s = jnp.where(lane == g, ps[0], jnp.where(lane == (g + 1) % 4, ps[1], jnp.where(lane == (g + 2) % 4, ps[2], 0.0)))
                if g:
                    s = pltpu.roll(s, 128 - 32 * g, 1)
                t32[pl.ds(pl.multiple_of(n * ROWS + g * G4 + r0, 16), 96), :] = s
            return 0
        lax.fori_loop(2 * half, 2 * half + 2, body, 0)

    started = set()

    def start_children(u, ox, oz):
        for i, m in enumerate(PLAN):
            if m[1] != u or i in started:
                continue
            sx, sz = (m[2] + m[5], m[3]) if m[4] == "x" else (m[2], m[3] + m[5])
            if (sx % NX, sz % NZ) == (ox % NX, oz % NZ):
                started.add(i)
                ag_copy(m, i).start()

    pack(0, 160)
    pl.semaphore_wait(barrier, len(peers))
    for u in (0, 1):
        start_children(u, 0, 0)
    pack(160, 224)
    for u in (2, 3):
        start_children(u, 0, 0)

    def icopy(k):
        return pltpu.make_async_remote_copy(src_ref=idx_own, dst_ref=idx_land.at[rep], send_sem=isend.at[k], recv_sem=irecv.at[k],
                                            device_id=dev("rep", k), device_id_type=MESH)
    for k in range(1, REP):
        icopy(k).start()
    idx_land[rep] = idx_own[...]
    work = [(0, 0, 0), (0, 0, 1)]
    for t in range(1, PLAN[-1][0] + 1):
        seen = []
        for i, m in enumerate(PLAN):
            if m[0] != t:
                continue
            ag_arrival(m, i).wait_recv()
            start_children(m[1], m[2], m[3])
            if (m[2] % NX, m[3] % NZ) not in seen:
                seen.append((m[2] % NX, m[3] % NZ))
            if work:
                ox, oz, half = work.pop(0)
                unpack(at(ox, oz), half)
        work += [(ox, oz, half) for ox, oz in seen for half in range(2)]
        if t == 2:
            for k in range(1, REP):
                icopy(k).wait_recv()
            to_smem = pltpu.make_async_copy(idx_land, idx_smem, lsem.at[3])
            to_smem.start()
    for ox, oz, half in work:
        unpack(at(ox, oz), half)
    to_smem.wait()

    def ocopy(k):
        return pltpu.make_async_remote_copy(src_ref=stage.at[k], dst_ref=got.at[rep], send_sem=osend.at[k], recv_sem=orecv.at[k],
                                            device_id=dev("rep", k), device_id_type=MESH)

    def arrived_slice(k):
        there = got.at[(rep - k + REP) % REP]
        return pltpu.make_async_remote_copy(src_ref=there, dst_ref=there, send_sem=osend.at[k], recv_sem=orecv.at[k],
                                            device_id=dev("rep", k), device_id_type=MESH)

    sums[200:208, :] = jnp.zeros((8, 128), jnp.float32)
    for k in list(range(1, REP)) + [0]:
        p = (rep + k) % REP

        def body(i, _):
            t = i // 4
            for half in range(2):
                b = i % 4 * 2 + half

                def row(q):
                    return t32[pl.ds(idx_smem[p, t, b, q], 1), :]
                for u in range(5):
                    rows = [row(u * F2 + q) for q in range(F2)]
                    while len(rows) > 1:
                        rows = [rows[a] + rows[a + 1] if a + 1 < len(rows) else rows[a] for a in range(0, len(rows), 2)]
                    sums[pl.ds(b * F1 + t * 5 + u, 1), :] = rows[0]
                    ones[pl.ds(b * F1 + t * 5 + u, 1), :] = row(75 + u)
            return 0
        lax.fori_loop(0, 4 * GROUPS, body, 0)
        for b in range(8):
            ones[pl.ds(200 + b, 1), :] = t32[pl.ds(idx_smem[p, 0, b, 80], 1), :]
        for h, part in ((0, sums[...] / F2), (1, ones[...])):
            if k:
                stage[k, 208 * h:208 * h + 208, :] = part.astype(jnp.bfloat16)
            else:
                got[rep, 208 * h:208 * h + 208, :] = part.astype(jnp.bfloat16)
        if k:
            ocopy(k).start()
    get_ws1.wait()
    get_wn1.wait()
    for k in range(1, REP):
        arrived_slice(k).wait_recv()
    counter = [0]

    def acc_row(part, row):
        return part * ROWS_G + row

    def new():
        counter[0] += 1
        return counter[0] - 1

    def copy(i, src, dst, axis, d):
        return pltpu.make_async_remote_copy(src_ref=src, dst_ref=dst, send_sem=send_sem.at[i], recv_sem=recv_sem.at[i],
                                            device_id=dev(axis, d), device_id_type=MESH)
    sent = []

    def send(i, src, dst, axis, d):
        c = copy(i, src, dst, axis, d)
        c.start()
        sent.append(c)

    def arrive(i, dst):
        copy(i, dst, dst, "c", 1).wait_recv()

    for ref, lo in ((ms, 0), (xs, 208)):
        lane = lax.broadcasted_iota(jnp.int32, (208, 128), 1)
        chunks = [None] * 6
        for r in range(REP):
            q, o = 96 * r // 128, 96 * r % 128
            v = got[r, lo:lo + 208, :].astype(jnp.float32)
            if o:
                v = pltpu.roll(v, o, 1)
            here = jnp.where(lane >= o, v, 0.0) if o > 32 else v
            chunks[q] = here if chunks[q] is None else chunks[q] + here
            if o > 32:
                chunks[q + 1] = jnp.where(lane < o, v, 0.0)
        for q in range(6):
            ref[:, 128 * q:128 * q + 128] = chunks[q].astype(jnp.bfloat16)
    r8 = lax.broadcasted_iota(jnp.int32, (8, 208), 0)
    c8 = lax.broadcasted_iota(jnp.int32, (8, 208), 1)
    pick = jnp.where((c8 < 200) & (c8 // F1 == r8), 1.0, 0.0).astype(jnp.bfloat16)
    mean_one = jnp.dot(pick, xs[...], preferred_element_type=jnp.float32) / F1
    ms[192:208, :] = jnp.concatenate([ms[192:208, :].astype(jnp.float32)[:8], mean_one], axis=0).astype(jnp.bfloat16)
    rr = lax.broadcasted_iota(jnp.int32, (208, 8), 0)
    cc = lax.broadcasted_iota(jnp.int32, (208, 8), 1)
    spread = jnp.where(jnp.where(rr < 200, rr // F1, rr - 200) == cc, 1.0, 0.0)
    ogs = jnp.dot(spread, og_ref[...].astype(jnp.float32), preferred_element_type=jnp.float32)
    row = lax.broadcasted_iota(jnp.int32, (208, C), 0)
    og_one = jnp.where(row < 200, ogs, 0.0).astype(jnp.bfloat16)
    og_seed = jnp.where(row < 200, 0.0, ogs).astype(jnp.bfloat16)
    TN = (((0,), (0,)), ((), ()))

    def grads(pair, put):
        cols = pl.ds(pl.multiple_of(pair * WIDE, WIDE), WIDE)
        pre = jnp.dot(xs[...], ws1[:, cols], preferred_element_type=jnp.float32) + jnp.dot(
            ms[...], wn1[:, cols], preferred_element_type=jnp.float32)
        s = 1.0 / (1.0 + jnp.exp(-pre))
        h = (pre * s).astype(jnp.bfloat16)
        d = jnp.dot(og_one, wn2[:, cols], preferred_element_type=jnp.float32) / F1 + jnp.dot(
            og_seed, ws2[:, cols], preferred_element_type=jnp.float32)
        g = (d * (s * (1.0 + pre * (1.0 - s)))).astype(jnp.bfloat16)
        put(0, 768, lax.dot_general(xs[...], g, TN, preferred_element_type=jnp.float32))
        put(768, 768, lax.dot_general(ms[...], g, TN, preferred_element_type=jnp.float32))
        put(GS2, C, lax.dot_general(og_seed, h, TN, preferred_element_type=jnp.float32))
        put(GN2, C, lax.dot_general(og_one, h, TN, preferred_element_type=jnp.float32) / F1)

    core_sem = [new() for _ in range(PARTS)]
    for pair in range(2):
        parts = (2 * pair, 2 * pair + 1)
        sib[2 * pair:2 * pair + 2, GS2:, :] = jnp.zeros((2, ROWS_G - GS2, 128), jnp.bfloat16)

        def put(lo, n, v):
            for c in range(2):
                sib[parts[c], lo:lo + n, :] = v[:, 128 * c:128 * c + 128].astype(jnp.bfloat16)
        grads((1 - core) * 2 + pair, put)
        for p in parts:
            send(core_sem[p], sib.at[p], crecv.at[p], "c", 1)

    def fold(part, row0, n, srcs):
        step = min(n, 128)

        def body(k, _):
            o = pl.multiple_of(k * step, 16)
            mine = pl.ds(pl.multiple_of(acc_row(part, row0 + o), 16), step)
            v = t32[mine, :]
            for ref in srcs:
                v = v + ref[pl.ds(o, step), :].astype(jnp.float32)
            t32[mine, :] = v
            sb[part, pl.ds(pl.multiple_of(row0 + o, 16), step), :] = v.astype(jnp.bfloat16)
            return 0
        lax.fori_loop(0, n // step, body, 0)

    def rows(ref, part, row0, n):
        return ref.at[part, pl.ds(pl.multiple_of(row0, 16), n)]

    class Ring:
        def __init__(self, part, axis, base, n, buf):
            self.part, self.axis, self.base, self.n, self.buf = part, axis, base, n, buf
            self.i = {"x": x, "y": y}[axis]
            self.sem = [new() for _ in range(6)]

        def q(self, k):
            return self.base + self.n * ((self.i + k) % 4)

        def go(self, m, row0, d):
            send(self.sem[m], rows(sb, self.part, row0, self.n // 2), self.buf.at[self.part, m], self.axis, d)

        def first(self):
            h = self.n // 2
            self.go(0, self.q(2), 1)
            self.go(2, self.q(2) + h, -1)
            self.go(1, self.q(1) + h, 1)
            self.go(3, self.q(3), -1)

        def second(self):
            h = self.n // 2
            for m, row0, d in ((0, self.q(1), 1), (2, self.q(3) + h, -1)):
                arrive(self.sem[m], self.buf.at[self.part, m])
                fold(self.part, row0, h, [self.buf.at[self.part, m]])
                self.go(4 + m // 2, row0, d)

        def last(self):
            h = self.n // 2
            for m in (3, 4, 1, 5):
                arrive(self.sem[m], self.buf.at[self.part, m])
            fold(self.part, self.q(0), h, [self.buf.at[self.part, 3], self.buf.at[self.part, 4]])
            fold(self.part, self.q(0) + h, h, [self.buf.at[self.part, 1], self.buf.at[self.part, 5]])

    axes = (("x", "y"), ("y", "x")) * (PARTS // 2)
    rings1 = []
    for pair in range(2):
        parts = (2 * pair, 2 * pair + 1)
        for p in parts:
            t32[acc_row(p, GS2):acc_row(p, ROWS_G), :] = jnp.zeros((ROWS_G - GS2, 128), jnp.float32)

        def put(lo, n, v):
            for c in range(2):
                t32[acc_row(parts[c], lo):acc_row(parts[c], lo) + n, :] = v[:, 128 * c:128 * c + 128]
        grads(core * 2 + pair, put)
        for p in parts:
            arrive(core_sem[p], crecv.at[p])
            fold(p, 0, ROWS_G, [crecv.at[p]])
            ring = Ring(p, axes[p][0], 0, 512, big)
            ring.first()
            rings1.append(ring)
    for ring in rings1:
        ring.second()
    rings2 = []
    for ring in rings1:
        ring.last()
        nxt = Ring(ring.part, axes[ring.part][1], ring.q(0), 128, small)
        nxt.first()
        rings2.append(nxt)
    for ring in rings2:
        ring.second()
    zsem = [[new() for _ in range(NZ - 1)] for _ in range(PARTS)]
    for ring in rings2:
        ring.last()
        for k in range(1, NZ):
            send(zsem[ring.part][k - 1], rows(sb, ring.part, ring.q(0) + 16 * ((z + k) % NZ), 16), tiny.at[ring.part, k - 1], "z", k)

    def final(part, row0, n):
        return fin.at[4 * core + part, pl.ds(pl.multiple_of(row0, 16), n)]

    fsem = [[new() for _ in range(NZ - 1)] for _ in range(PARTS)]
    for ring in rings2:
        p = ring.part
        for k in range(1, NZ):
            arrive(zsem[p][k - 1], tiny.at[p, k - 1])
        r0 = pl.multiple_of(ring.q(0) + 16 * z, 16)
        v = t32[pl.ds(pl.multiple_of(acc_row(p, r0), 16), 16), :]
        for k in range(NZ - 1):
            v = v + tiny[p, k].astype(jnp.float32)
        fin[4 * core + p, pl.ds(r0, 16), :] = v.astype(jnp.bfloat16)
        for k in range(1, NZ):
            here = final(p, r0, 16)
            send(fsem[p][k - 1], here, here, "z", k)

    def spread_first(part, axis, base, n, i, sem):
        here = final(part, base + n * i, n)
        send(sem[0], here, here, axis, 1)
        send(sem[1], here, here, axis, -1)

    def spread_second(part, axis, base, n, i, sem):
        h = n // 2
        a = base + n * ((i + 3) % 4)
        arrive(sem[0], final(part, a, n))
        here = final(part, a, h)
        send(sem[2], here, here, axis, 1)
        b = base + n * ((i + 1) % 4)
        arrive(sem[1], final(part, b, n))
        here = final(part, b + h, h)
        send(sem[3], here, here, axis, -1)
        return a, b

    def spread_last(part, axis, base, n, i, sem):
        o = base + n * ((i + 2) % 4)
        arrive(sem[2], final(part, o, n // 2))
        arrive(sem[3], final(part, o + n // 2, n // 2))
        return o

    sems = [[new() for _ in range(4)] for _ in range(PARTS)]
    for ring in rings2:
        for k in range(1, NZ):
            arrive(fsem[ring.part][k - 1], final(ring.part, ring.q(0) + 16 * ((z - k + NZ) % NZ), 16))
        spread_first(ring.part, ring.axis, ring.base, 128, ring.i, sems[ring.part])
    for ring in rings2:
        spread_second(ring.part, ring.axis, ring.base, 128, ring.i, sems[ring.part])
    sems1 = [[new() for _ in range(4)] for _ in range(PARTS)]
    csem = [[new() for _ in range(4)] for _ in range(PARTS)]

    def across(part, k, row0):
        here = final(part, row0, 512)
        send(csem[part][k], here, here, "c", 1)

    for ring in rings2:
        p = ring.part
        spread_last(p, ring.axis, ring.base, 128, ring.i, sems[p])
        spread_first(p, axes[p][0], 0, 512, rings1[p].i, sems1[p])
        across(p, 0, rings1[p].q(0))
    for ring in rings1:
        p = ring.part
        a, b = spread_second(p, ring.axis, 0, 512, ring.i, sems1[p])
        across(p, 1, a)
        across(p, 2, b)
    for ring in rings1:
        p = ring.part
        across(p, 3, spread_last(p, ring.axis, 0, 512, ring.i, sems1[p]))
    outs = []

    def deliver(n, h):
        cols = pl.ds(pl.multiple_of(128 * h, 128), 128)
        for m, (ref, lo) in enumerate(((gs1, 0), (gn1, 768))):
            outs.append(pltpu.make_async_copy(fin.at[h, pl.ds(lo, 768)], ref.at[:, cols], lsem.at[4 + 2 * n + m]))
            outs[-1].start()
        for ref, lo in ((gs2, GS2), (gn2, GN2)):
            ref[:, cols] = fin[h, lo:lo + C, :]

    for p in range(PARTS):
        deliver(p, 4 * core + p)
    for ring in rings1:
        p = ring.part
        for k, off in enumerate((0, 3, 1, 2)):
            here = fin.at[4 * (1 - core) + p, pl.ds(pl.multiple_of(ring.q(off), 16), 512)]
            arrive(csem[p][k], here)
        deliver(PARTS + p, 4 * (1 - core) + p)
    assert counter[0] == N_SEM, counter[0]
    for c in outs:
        c.wait()
    for c in sent:
        c.wait_send()
    for k in range(1, REP):
        ocopy(k).wait_send()
        icopy(k).wait_send()
    for i, m in enumerate(PLAN):
        ag_copy(m, i).wait_send()


def per_device(
    table, near_owner, near_row, far_owner, far_row, w_self1, w_neigh1, w_self2, w_neigh2, out_grad
):
    bf, f32, n = jnp.bfloat16, jnp.float32, len(PLAN)
    vmem, hbm, dma = pl.BlockSpec(memory_space=pltpu.VMEM), pl.BlockSpec(memory_space=pl.ANY), pltpu.SemaphoreType.DMA
    turned = [w_self2.T, w_neigh2.T]
    out = pl.pallas_call(
        kernel,
        out_shape=[jax.ShapeDtypeStruct(a.shape, bf) for a in (w_self1, w_neigh1, *turned)],
        in_specs=[vmem] * 4 + [hbm] * 3 + [vmem] * 3,
        out_specs=[hbm, hbm, vmem, vmem],
        scratch_shapes=[
            pltpu.VMEM((ROWS, 256), bf),
            pltpu.VMEM((NZ * NX, G4, 384), bf),
            pltpu.VMEM((NZ * NX * ROWS, 128), f32),
            pltpu.VMEM((208, 128), f32),
            pltpu.VMEM((208, 128), f32),
            pltpu.VMEM((REP, 416, 128), bf),
            pltpu.VMEM((REP, 416, 128), bf),
            pltpu.VMEM((GROUPS, 8, 128), jnp.int32),
            pltpu.VMEM((REP, GROUPS, 8, 128), jnp.int32),
            pltpu.SMEM((REP, GROUPS, 8, 128), jnp.int32),
            pltpu.VMEM((768, 1024), bf),
            pltpu.VMEM((768, 1024), bf),
            pltpu.VMEM((208, 768), bf),
            pltpu.VMEM((208, 768), bf),
            pltpu.VMEM((PARTS, ROWS_G, 128), bf),
            pltpu.VMEM((PARTS, ROWS_G, 128), bf),
            pltpu.VMEM((PARTS, ROWS_G, 128), bf),
            pltpu.VMEM((PARTS, 6, 256, 128), bf),
            pltpu.VMEM((PARTS, 6, 64, 128), bf),
            pltpu.VMEM((PARTS, 7, 16, 128), bf),
            pltpu.VMEM((8, ROWS_G, 128), bf),
            dma((n,)), dma((n,)), dma((REP,)), dma((REP,)), dma((REP,)), dma((REP,)), dma((N_SEM,)), dma((N_SEM,)), dma((20,)),
        ],
        compiler_params=pltpu.CompilerParams(collective_id=0, has_side_effects=True, vmem_limit_bytes=61 * 10**6),
        cost_estimate=pl.CostEstimate(flops=4 * 10**9, bytes_accessed=3 * 10**7, transcendentals=0),
        name="step",
    )(near_owner.reshape(near_row.shape), near_row, far_owner.reshape(far_row.shape), far_row, table,
      w_self1, w_neigh1, *turned, out_grad)
    return out[0], out[1], out[2].T, out[3].T


def solution(mesh):
    rows = P(("node", "rep"))
    return jax.shard_map(
        per_device,
        mesh=mesh,
        in_specs=(P("node"), rows, rows, rows, rows, P(), P(), P(), P(), rows),
        out_specs=(P(), P(), P(), P()),
        check_vma=False,
    )
```
